32 devices in a mesh: grp: 2 (over y), dev: 16 (over z, x, core).
Axes of the slice: x: 2, y: 2, z: 4, core: 2. Of those that a mesh axis runs over, the one named last changes fastest.
Arguments:
- embeddings: bfloat16 [12288, 768], P(('grp', 'dev')), may hold values from -6 to 6
- labels: bfloat16 [12288, 896], P(('grp', 'dev')), may hold values from -6 to 6
- cluster_rows: int32 [32], P(('grp', 'dev')), may hold values from 96 to 384, as said below
Outputs:
- propagated: bfloat16 [12288, 896], P(('grp', 'dev'))
The draws below stay inside these ranges and needn't reach their ends.
Inputs may be any that keep to these rules, and one draw needn't show every extreme that they name: `cluster_rows`: some cluster has all 384 slots filled and some has 96.
All inputs are finite; a program needn't handle non-finite values.
Results may differ from the reference program's by a relative error of at most 0.006.
Values may be sent and summed in bfloat16 or wider, within the bound.
No kernel may reach another device: no remote copies, remote signals or barrier semaphores. Data moves between devices by JAX's collectives and lax.ppermute only.
A program may use at most 64 MiB of HBM per device.

```python
import math
import jax
import jax.numpy as jnp
from jax import lax

D = 768
C = 896
ROWS = 384
INNER = 4
GROUPS = 2
OWNERS = 16
CLUSTERS = 32
TOTAL_ROWS = 12288


def draw_cluster_rows(key, part):
    key = jax.random.fold_in(key, 11)
    first_key, second_key = jax.random.split(key)
    counts = jax.random.randint(first_key, (CLUSTERS,), ROWS // 4, ROWS + 1)
    order = jax.random.permutation(second_key, CLUSTERS)
    counts = counts.at[order[0]].set(ROWS)
    counts = counts.at[order[1]].set(ROWS // 4)
    return counts.astype(jnp.int32)


def shard_levels(stream_key, shape, cuts, smallest, largest):
    def one(dim, parts):
        draws = jax.random.uniform(jax.random.fold_in(jax.random.fold_in(stream_key, 6), dim), (parts,), jnp.float32, smallest / len(cuts), largest / len(cuts))
        return jnp.repeat(jnp.exp(draws), shape[dim] // parts).reshape((-1,) + (1,) * (len(shape) - dim - 1))

    level = one(*cuts[0])
    for cut in cuts[1:]:
        level = level * one(*cut)
    return level


def noise(key, shape, deviation, reach, pieces=(), held_as=jnp.bfloat16):
    drawn = deviation * jax.random.normal(key, shape, jnp.float32)
    if pieces:
        drawn = drawn * shard_levels(key, shape, pieces, -0.22, 0.18)
    return jnp.clip(drawn, -reach, reach).astype(held_as)


def setup_inputs(seed: int = 0) -> dict:
    splits = jax.random.split(jax.random.key(seed), 4)
    embeddings = noise(splits[0], (TOTAL_ROWS, D), 1.0, 6.0, ((0, 32),))
    labels = noise(splits[1], (TOTAL_ROWS, C), 1.0, 6.0, ((0, 32),))
    cluster_rows = draw_cluster_rows(jax.random.fold_in(splits[3], 71), 0)
    return dict(embeddings=embeddings, labels=labels, cluster_rows=cluster_rows)


sharpness = 25.0
keep_share = 0.8

def unit_rows(embeddings):
    values = embeddings.astype(jnp.float32)
    scaled = values * lax.rsqrt(lax.optimization_barrier(jnp.mean(values * values, axis=-1, keepdims=True)) + 1e-06)
    return (scaled / math.sqrt(values.shape[-1])).astype(jnp.bfloat16)

def raw_affinity(left_unit, right_unit):
    cosine = jnp.dot(left_unit, right_unit.T, preferred_element_type=jnp.float32)
    return jnp.exp(sharpness * cosine)

def reference(embeddings, labels, cluster_rows):
    label_shape = (GROUPS, OWNERS, ROWS, C)
    unit_vectors = unit_rows(embeddings).reshape(GROUPS, OWNERS, ROWS, D)
    places = lax.iota(jnp.int32, ROWS)
    row_valid = (places[None, :] < cluster_rows[:, None]).astype(jnp.float32).reshape(GROUPS, OWNERS, ROWS, 1)
    seed_labels = labels.reshape(label_shape) * row_valid.astype(jnp.bfloat16)
    offdiag = (places[:, None] != places[None, :]).astype(jnp.float32)

    def flatten(array):
        return array.reshape((CLUSTERS,) + array.shape[2:])

    def self_term(operands):
        left_unit, own_labels = operands
        pair_tile = (raw_affinity(left_unit, left_unit) * offdiag).astype(jnp.bfloat16)
        return jnp.dot(pair_tile, own_labels, preferred_element_type=jnp.float32)

    def pair_terms(operands):
        left_unit, right_unit, own_labels, far_labels = operands
        pair_tile = raw_affinity(left_unit, right_unit).astype(jnp.bfloat16)
        forward = jnp.dot(pair_tile, far_labels, preferred_element_type=jnp.float32)
        backward = jnp.dot(pair_tile.T, own_labels, preferred_element_type=jnp.float32)
        return (forward, backward)
    offsets = [(1, stride) for stride in range(1, INNER + 1)] + [(0, 1)]
    current = seed_labels
    for sweep_index in range(2):
        summed = lax.map(self_term, (flatten(unit_vectors), flatten(current))).reshape(label_shape)
        for axis_number, stride in offsets:
            right_unit = jnp.roll(unit_vectors, -stride, axis=axis_number)
            far_labels = jnp.roll(current, -stride, axis=axis_number)
            forward, backward = lax.map(pair_terms, (flatten(unit_vectors), flatten(right_unit), flatten(current), flatten(far_labels)))
            summed = summed + forward.reshape(label_shape)
            summed = summed + jnp.roll(backward.reshape(label_shape), stride, axis=axis_number)
        factor = lax.rsqrt(lax.optimization_barrier(jnp.mean(summed * summed, axis=-1, keepdims=True)) + 1e-06)
        mixed = keep_share * summed * factor + (1.0 - keep_share) * seed_labels.astype(jnp.float32)
        current = (mixed * row_valid).astype(jnp.bfloat16)
    return current.reshape(TOTAL_ROWS, C)
```

```python
import functools
import math

import jax
import jax.numpy as jnp
from jax import lax
from jax.experimental import pallas as pl
from jax.experimental.pallas import tpu as pltpu
from jax.sharding import PartitionSpec as P

sharpness = 25.0
keep_share = 0.8
BF16 = jnp.bfloat16
F32 = jnp.float32
QUAD = 4
INVALID = 1e38
MB = 2**20


def along_dev(block, source):
    size = lax.axis_size("dev")
    return lax.ppermute(block, "dev", [(source(i) % size, i) for i in range(size)])


def from_up(block):
    return along_dev(block, lambda i: i + QUAD)


def from_down(block):
    return along_dev(block, lambda i: i - QUAD)


def from_side(block):
    return along_dev(block, lambda i: i ^ 2)


def from_core(block):
    return along_dev(block, lambda i: i ^ 1)


def from_group(block, step):
    size = lax.axis_size("grp")
    return lax.ppermute(block, "grp", [((i + step) % size, i) for i in range(size)])


def after(value, earlier):
    return lax.optimization_barrier((value, earlier))[0]


def exchange(pieces):
    return [along_dev(piece, lambda i, m=m: i ^ m) for m, piece in enumerate(pieces, 1)]


def call(kernel, name, operands, out_shape, scratch=(), limit=24):
    specs = [
        pl.BlockSpec(memory_space=pltpu.SMEM if x.dtype == jnp.int32 else pltpu.VMEM) for x in operands
    ]
    return pl.pallas_call(
        kernel,
        in_specs=specs,
        out_shape=out_shape,
        scratch_shapes=list(scratch),
        compiler_params=pltpu.CompilerParams(vmem_limit_bytes=limit * MB),
        name=name,
    )(*operands)


def like(shape, dtype):
    return jax.ShapeDtypeStruct(tuple(shape), dtype)


def dot(left, right):
    return jnp.dot(left, right, preferred_element_type=F32)


def affinity(left, right):
    cosine = lax.dot_general(left, right, (((1,), (1,)), ((), ())), preferred_element_type=F32)
    return jnp.exp2(cosine * (sharpness * math.log2(math.e)))


def cut(block, place, pieces):
    quarter = block.shape[1] // QUAD
    for k in range(QUAD):
        for m, piece in pieces:

            @pl.when(place ^ m == k)
            def _():
                piece[...] = block[:, k * quarter : (k + 1) * quarter]


def join(place, pieces, out):
    quarter = out.shape[1] // QUAD
    for k in range(QUAD):
        for m, piece in pieces:

            @pl.when(place ^ m == k)
            def _():
                out[:, k * quarter : (k + 1) * quarter] = piece[...]


def unit_kernel(embeddings, unit):
    values = embeddings[...].astype(F32)
    scaled = values * lax.rsqrt(jnp.mean(values * values, axis=-1, keepdims=True) + 1e-06)
    unit[...] = (scaled / math.sqrt(values.shape[-1])).astype(BF16)


def seed_kernel(scalars, labels, seed, *pieces):
    row = lax.broadcasted_iota(jnp.int32, labels.shape, 0)
    seed[...] = jnp.where(row < scalars[1], labels[...].astype(F32), 0.0).astype(BF16)
    cut(seed, scalars[0], list(enumerate(pieces, 1)))


def pack_kernel(scalars, whole, *rest):
    pieces, out = rest[:-1], rest[-1]
    out[...] = whole[...]
    join(scalars[0], list(enumerate(pieces, 1)), out)


def at(cluster, rows):
    return pl.ds(pl.multiple_of(cluster * rows, rows), rows)


def near_kernel(clusters, own, side, core, across, units, near):
    rows = own.shape[0]
    for i, block in enumerate((own, side, core, across)):
        units[at(clusters[i], rows), :] = block[...]
    for k in range(QUAD):
        for pair in range(2):
            span = slice(2 * pair * rows, 2 * (pair + 1) * rows)
            tile = affinity(units[k * rows : (k + 1) * rows, :], units[span, :])
            if k // 2 == pair:
                row = lax.broadcasted_iota(jnp.int32, tile.shape, 0)
                lane = lax.broadcasted_iota(jnp.int32, tile.shape, 1)
                tile = jnp.where(row + (k % 2) * rows == lane, 0.0, tile)
            near[k * rows : (k + 1) * rows, span] = tile.astype(BF16)


def far_kernel(clusters, units, up, side, core, across, own, far, sums, up_units, stack):
    rows = up.shape[0]
    for i, block in enumerate((up, core, side, across)):
        up_units[at(clusters[(0, 2, 1, 3)[i]], rows), :] = block[...]
    unpack(own, stack)
    for k in range(QUAD):
        here = slice(k * rows, (k + 1) * rows)
        for first in range(0, k + 1, 2):
            span = slice(first * rows, min(first + 2, k + 1) * rows)
            far[here, span] = affinity(units[here, :], up_units[span, :]).astype(BF16)
    scatter(far, stack, sums)


def unpack(block, stack):
    rows, quarter = stack.shape[0] // QUAD, stack.shape[1]
    for k in range(QUAD):
        stack[k * rows : (k + 1) * rows, :] = block[:, k * quarter : (k + 1) * quarter]


def scatter(far, stack, out):
    rows, quarter = stack.shape[0] // QUAD, stack.shape[1]
    for k in range(QUAD):
        total = lax.dot_general(
            far[k * rows :, k * rows : (k + 1) * rows],
            stack[k * rows :, :],
            (((0,), (0,)), ((), ())),
            preferred_element_type=F32,
        )
        out[:, k * quarter : (k + 1) * quarter] = total.astype(out.dtype)


def scatter_kernel(scalars, far, own, out, *rest):
    pieces, stack = rest[:-1], rest[-1]
    unpack(own, stack)
    scatter(far, stack, out)
    cut(out, scalars[0], list(enumerate(pieces, 1)))


def cross_kernel(weight, unit, *rest):
    others, out = rest[:-1], rest[-1]
    rows = unit.shape[0]
    for n, other in enumerate(others):
        out[n * rows : (n + 1) * rows, :] = (affinity(unit[...], other[...]) * weight).astype(BF16)


def gather_kernel(crosses, clusters, near, far, t0, t1, t2, t3, own, up, *rest):
    cross, (out, *pieces, stack, total) = rest[:crosses], rest[crosses:]
    rows, quarter = own.shape[0], own.shape[1] // QUAD
    unpack(own, stack)
    for k in range(QUAD):
        here = slice(k * rows, (k + 1) * rows)
        total[here, :] = dot(near[here, :], stack[...])
    for n, block in enumerate(cross):
        unpack(block, stack)
        for i, tile in enumerate((t0, t1, t2, t3)):
            here = at(clusters[i], rows)
            total[here, :] += dot(tile[n * rows : (n + 1) * rows, :], stack[here, :])
    unpack(up, stack)
    for k in range(QUAD):
        here = slice(k * rows, (k + 1) * rows)
        done = total[here, :] + dot(far[here, : (k + 1) * rows], stack[: (k + 1) * rows, :])
        out[:, k * quarter : (k + 1) * quarter] = done.astype(out.dtype)
    cut(out, clusters[0], list(enumerate(pieces, 1)))


def lanes_of(cluster_count, lanes):
    quarter = lanes // QUAD
    row = lax.broadcasted_iota(jnp.int32, (cluster_count, lanes), 0)
    lane = lax.broadcasted_iota(jnp.int32, (cluster_count, lanes), 1)
    return ((lane >= row * quarter) & (lane < (row + 1) * quarter)).astype(F32)


def combine_kernel(scalars, kept, sent, summed, squares):
    total = kept[...] + sent[...].astype(F32)
    summed[...] = total
    sums = lax.dot_general(
        lanes_of(8, total.shape[1]),
        total * total,
        (((1,), (1,)), ((), ())),
        precision=lax.Precision.HIGHEST,
        preferred_element_type=F32,
    )
    row = lax.broadcasted_iota(jnp.int32, sums.shape, 0)
    lane = lax.broadcasted_iota(jnp.int32, sums.shape, 1)
    squares[...] = sums + jnp.where((row == scalars[0]) & (lane >= scalars[1]), INVALID, 0.0)


def mix_kernel(summed, s0, s1, s2, s3, seed, out):
    total = (s0[...] + s1[...]) + (s2[...] + s3[...])
    factor = jnp.where(total > INVALID / 10, 0.0, lax.rsqrt(total / summed.shape[1] + 1e-06))
    spread = lax.dot_general(
        factor,
        lanes_of(8, summed.shape[1]),
        (((0,), (0,)), ((), ())),
        precision=lax.Precision.HIGHEST,
        preferred_element_type=F32,
    )
    out[...] = (keep_share * summed[...] * spread + (1.0 - keep_share) * seed[...].astype(F32)).astype(BF16)


def finish_kernel(scalars, kept, k1, k2, k3, sent, seed, out, whole):
    whole[...] = kept[...]
    join(scalars[0], [(1, k1), (2, k2), (3, k3)], whole)
    summed = whole[...].astype(F32) + sent[...].astype(F32)
    factor = lax.rsqrt(jnp.mean(summed * summed, axis=-1, keepdims=True) + 1e-06)
    result = keep_share * summed * factor + (1.0 - keep_share) * seed[...].astype(F32)
    row = lax.broadcasted_iota(jnp.int32, summed.shape, 0)
    out[...] = jnp.where(row < scalars[1], result, 0.0).astype(BF16)


def body(embeddings, labels, cluster_rows):
    rows, classes = labels.shape
    depth = embeddings.shape[1]
    groups = lax.axis_size("grp")
    steps, weight = ([1], 2.0) if groups == 2 else ([1, -1], 1.0)
    place = (lax.axis_index("dev") % QUAD).astype(jnp.int32)
    clusters = jnp.stack([place, place ^ 2, place ^ 1, place ^ 3])
    scalars = jnp.stack([place, cluster_rows[0]])
    stack = pltpu.VMEM((QUAD * rows, classes // QUAD), BF16)
    total = pltpu.VMEM((QUAD * rows, classes // QUAD), F32)
    packed = like(labels.shape, BF16)
    piece = like((rows, classes // QUAD), BF16)
    matrix = like((QUAD * rows, QUAD * rows), BF16)

    unit = call(unit_kernel, "unit", (embeddings,), like(embeddings.shape, BF16))
    unit_up = from_up(unit)
    seed, *pieces = call(seed_kernel, "seed", (scalars, labels), (packed, piece, piece, piece))
    received = exchange(pieces)
    unit_side, unit_core = from_side(unit), from_core(unit)
    cross_unit = [from_group(unit, step) for step in steps]
    received[0] = after(received[0], unit_up)
    packed_seed = call(pack_kernel, "pack", (scalars, seed, *received), packed)
    seed_up = from_up(packed_seed)
    seed_cross = [from_group(packed_seed, step) for step in steps]
    up_side, up_core = from_side(unit_up), from_core(unit_up)
    cross0 = call(
        functools.partial(cross_kernel, weight), "cross", (unit, *cross_unit), like((len(steps) * rows, rows), BF16)
    )
    unit_side = after(unit_side, packed_seed)
    unit_across = from_core(unit_side)
    unit_side = after(unit_side, cross0)
    units, near = call(
        near_kernel,
        "near",
        (clusters, unit, unit_side, unit_core, unit_across),
        (like((QUAD * rows, depth), BF16), matrix),
    )
    up_side = after(up_side, units)
    up_across = from_core(up_side)
    cross0 = after(cross0, up_side)
    cross1, cross2 = from_side(cross0), from_core(cross0)
    cross3 = from_core(cross1)
    up_core = after(up_core, seed_up)
    far, sums = call(
        far_kernel,
        "far",
        (clusters, units, unit_up, up_side, up_core, up_across, packed_seed),
        (matrix, packed),
        [pltpu.VMEM((QUAD * rows, depth), BF16), stack],
        limit=28,
    )

    def gather(own, up, cross, out):
        return call(
            functools.partial(gather_kernel, len(cross)),
            "gather",
            (clusters, near, far, cross0, cross1, cross2, cross3, own, up, *cross),
            out,
            [stack, total],
        )

    sent = from_down(sums)
    kept = gather(packed_seed, seed_up, seed_cross, like(labels.shape, F32))
    summed, squares = call(
        combine_kernel, "combine", (scalars, kept, sent), (like(labels.shape, F32), like((8, rows), F32))
    )
    current = call(mix_kernel, "mix", (summed, squares, *exchange([squares] * 3), packed_seed), packed)

    current_up = from_up(current)
    current_cross = [from_group(current, step) for step in steps]
    sums, *pieces = call(
        scatter_kernel, "scatter", (scalars, far, current), (packed, piece, piece, piece), [stack]
    )
    sums = call(pack_kernel, "pack", (scalars, sums, *exchange(pieces)), packed)
    sent = from_down(sums)
    current_up = after(current_up, sums)
    kept, *pieces = gather(current, current_up, current_cross, (packed, piece, piece, piece))
    return call(
        finish_kernel, "finish", (scalars, kept, *exchange(pieces), sent, seed), packed, [pltpu.VMEM(labels.shape, BF16)]
    )


def solution(mesh):
    placed = (P(("grp", "dev"), None), P(("grp", "dev"), None), P(("grp", "dev")))
    return jax.shard_map(
        body, mesh=mesh, in_specs=placed, out_specs=P(("grp", "dev"), None), check_vma=False
    )
```

```python
import functools
import math

import jax
import jax.numpy as jnp
from jax import lax
from jax.experimental import pallas as pl
from jax.experimental.pallas import tpu as pltpu
from jax.sharding import PartitionSpec as P

sharpness = 25.0
keep_share = 0.8
BF16 = jnp.bfloat16
F32 = jnp.float32
QUAD = 4
INVALID = 1e38
MB = 2**20


def along_dev(block, source):
    size = lax.axis_size("dev")
    return lax.ppermute(block, "dev", [(source(i) % size, i) for i in range(size)])


def from_up(block):
    return along_dev(block, lambda i: i + QUAD)


def from_down(block):
    return along_dev(block, lambda i: i - QUAD)


def from_side(block):
    return along_dev(block, lambda i: i ^ 2)


def from_core(block):
    return along_dev(block, lambda i: i ^ 1)


def from_group(block, step):
    size = lax.axis_size("grp")
    return lax.ppermute(block, "grp", [((i + step) % size, i) for i in range(size)])


def after(value, earlier):
    return lax.optimization_barrier((value, earlier))[0]


def exchange(pieces):
    return [along_dev(piece, lambda i, m=m: i ^ m) for m, piece in enumerate(pieces, 1)]


def call(kernel, name, operands, out_shape, scratch=(), limit=12, aliases={}):
    specs = [
        pl.BlockSpec(memory_space=pltpu.SMEM if x.dtype == jnp.int32 else pltpu.VMEM) for x in operands
    ]
    return pl.pallas_call(
        kernel,
        in_specs=specs,
        out_shape=out_shape,
        scratch_shapes=list(scratch),
        input_output_aliases=aliases,
        compiler_params=pltpu.CompilerParams(vmem_limit_bytes=limit * MB),
        name=name,
    )(*operands)


def like(shape, dtype):
    return jax.ShapeDtypeStruct(tuple(shape), dtype)


def dot(left, right):
    return jnp.dot(left, right, preferred_element_type=F32)


def affinity(left, right):
    cosine = lax.dot_general(left, right, (((1,), (1,)), ((), ())), preferred_element_type=F32)
    return jnp.exp2(cosine * (sharpness * math.log2(math.e)))


def cut(block, place, pieces):
    quarter = block.shape[1] // QUAD
    for k in range(QUAD):
        for m, piece in pieces:

            @pl.when(place ^ m == k)
            def _():
                piece[...] = block[:, k * quarter : (k + 1) * quarter]


def join(place, pieces, out):
    quarter = out.shape[1] // QUAD
    for k in range(QUAD):
        for m, piece in pieces:

            @pl.when(place ^ m == k)
            def _():
                out[:, k * quarter : (k + 1) * quarter] = piece[...]


def unit_kernel(embeddings, unit, *parts):
    values = embeddings[...].astype(F32)
    scaled = values * lax.rsqrt(jnp.mean(values * values, axis=-1, keepdims=True) + 1e-06)
    unit[...] = (scaled / math.sqrt(values.shape[-1])).astype(BF16)
    halve(unit, parts)


def halve(block, parts):
    first = 0
    for part in parts:
        part[...] = block[first : first + part.shape[0], :]
        first = first + part.shape[0]


def seed_kernel(scalars, labels, seed, *pieces):
    row = lax.broadcasted_iota(jnp.int32, labels.shape, 0)
    seed[...] = jnp.where(row < scalars[1], labels[...].astype(F32), 0.0).astype(BF16)
    cut(seed, scalars[0], list(enumerate(pieces, 1)))


def pack_kernel(scalars, whole, p1, p2, p3, out, *parts):
    out[...] = whole[...]
    join(scalars[0], [(1, p1), (2, p2), (3, p3)], out)
    halve(out, parts)


def at(cluster, rows):
    return pl.ds(pl.multiple_of(cluster * rows, rows), rows)


def place_rows(cluster, blocks, rows, stack):
    start = cluster * rows
    for block in blocks:
        count = block.shape[0]
        stack[pl.ds(pl.multiple_of(start, count), count), :] = block[...]
        start = start + count


def near_kernel(units, near):
    rows = units.shape[0] // QUAD
    for k in range(QUAD):
        for pair in range(2):
            span = slice(2 * pair * rows, 2 * (pair + 1) * rows)
            tile = affinity(units[k * rows : (k + 1) * rows, :], units[span, :])
            if k // 2 == pair:
                row = lax.broadcasted_iota(jnp.int32, tile.shape, 0)
                lane = lax.broadcasted_iota(jnp.int32, tile.shape, 1)
                tile = jnp.where(row + (k % 2) * rows == lane, 0.0, tile)
            near[k * rows : (k + 1) * rows, span] = tile.astype(BF16)


def stage_kernel(clusters, unit, side_a, core, across_a, up, up_side_a, up_core, up_across_a, own, units, up_units, stack):
    rows = unit.shape[0]
    for i, (mine, upper) in enumerate(
        ((unit, up), (side_a, up_side_a), (core, up_core), (across_a, up_across_a))
    ):
        place_rows(clusters[i], (mine,), rows, units)
        place_rows(clusters[i], (upper,), rows, up_units)
    unpack(own, stack)


def far_kernel(clusters, units_in, up_in, side_b, across_b, stack, units, up_units, far, sums):
    rows = units.shape[0] // QUAD
    half = rows // 2
    for i, block in ((1, side_b), (3, across_b)):
        start = pl.multiple_of(clusters[i] * rows + half, half)
        units[pl.ds(start, half), :] = block[:half, :]
        up_units[pl.ds(start, half), :] = block[half:, :]
    for k in range(QUAD):
        here = slice(k * rows, (k + 1) * rows)
        for first in range(0, k + 1, 2):
            span = slice(first * rows, min(first + 2, k + 1) * rows)
            far[here, span] = affinity(units[here, :], up_units[span, :]).astype(BF16)
    scatter(far, stack, sums)


def unpack(block, stack):
    rows, quarter = stack.shape[0] // QUAD, stack.shape[1]
    for k in range(QUAD):
        stack[k * rows : (k + 1) * rows, :] = block[:, k * quarter : (k + 1) * quarter]


def scatter(far, stack, out):
    rows, quarter = stack.shape[0] // QUAD, stack.shape[1]
    for k in range(QUAD):
        total = lax.dot_general(
            far[k * rows :, k * rows : (k + 1) * rows],
            stack[k * rows :, :],
            (((0,), (0,)), ((), ())),
            preferred_element_type=F32,
        )
        out[:, k * quarter : (k + 1) * quarter] = total.astype(out.dtype)


def mix_kernel(scalars, far, summed, s0, s1, s2, s3, seed, factor, mixed, stack, out, p1, p2, p3):
    total = (s0[...] + s1[...]) + (s2[...] + s3[...])
    factor[...] = jnp.where(total > INVALID / 10, 0.0, lax.rsqrt(total / summed.shape[1] + 1e-06))
    mixed[...] = mix(summed, factor, seed)
    unpack(mixed, stack)
    scatter(far, stack, out)
    cut(out, scalars[0], [(1, p1), (2, p2), (3, p3)])


def cross_kernel(weight, unit, *rest):
    others, out = rest[:-1], rest[-1]
    rows = unit.shape[0]
    for n, other in enumerate(others):
        out[n * rows : (n + 1) * rows, :] = (affinity(unit[...], other[...]) * weight).astype(BF16)


def near_products(near, stack, total):
    rows = stack.shape[0] // QUAD
    for k in range(QUAD):
        here = slice(k * rows, (k + 1) * rows)
        total[here, :] = dot(near[here, :], stack[...])


def cross_products(clusters, tiles, n, stack, total):
    rows = stack.shape[0] // QUAD
    for i, tile in enumerate(tiles):
        here = at(clusters[i], rows)
        total[here, :] += dot(tile[n * rows : (n + 1) * rows, :], stack[here, :])


def far_products(far, stack, total, out):
    rows, quarter = stack.shape[0] // QUAD, stack.shape[1]
    for k in range(QUAD):
        here = slice(k * rows, (k + 1) * rows)
        done = total[here, :] + dot(far[here, : (k + 1) * rows], stack[: (k + 1) * rows, :])
        out[:, k * quarter : (k + 1) * quarter] = done.astype(out.dtype)


def gather_kernel(clusters, near, far, t0, t1, t2, t3, own, up, *rest):
    cross, (out, stack, total) = rest[:-3], rest[-3:]
    unpack(own, stack)
    near_products(near, stack, total)
    for n, block in enumerate(cross):
        unpack(block, stack)
        cross_products(clusters, (t0, t1, t2, t3), n, stack, total)
    unpack(up, stack)
    far_products(far, stack, total, out)


def gather_mixed_kernel(clusters, far, t0, t1, t2, t3, total_in, *rest):
    triples, (total, out, p1, p2, p3, mixed, stack) = rest[:-7], rest[-7:]
    triples = [triples[i : i + 3] for i in range(0, len(triples), 3)]
    for n, (summed, factor, seed) in enumerate(triples[1:]):
        mixed[...] = mix(summed, factor, seed)
        unpack(mixed, stack)
        cross_products(clusters, (t0, t1, t2, t3), n, stack, total)
    mixed[...] = mix(*triples[0])
    unpack(mixed, stack)
    far_products(far, stack, total, out)
    cut(out, clusters[0], [(1, p1), (2, p2), (3, p3)])


def lanes_of(lanes):
    quarter = lanes // QUAD
    row = lax.broadcasted_iota(jnp.int32, (8, lanes), 0)
    lane = lax.broadcasted_iota(jnp.int32, (8, lanes), 1)
    return ((lane >= row * quarter) & (lane < (row + 1) * quarter)).astype(F32)


def mix(summed, factor, seed):
    spread = lax.dot_general(
        factor[...],
        lanes_of(summed.shape[1]),
        (((0,), (0,)), ((), ())),
        precision=lax.Precision.HIGHEST,
        preferred_element_type=F32,
    )
    share = keep_share * summed[...].astype(F32) * spread
    return (share + (1.0 - keep_share) * seed[...].astype(F32)).astype(BF16)


def combine_kernel(scalars, kept, sent, summed, squares):
    total = kept[...] + sent[...].astype(F32)
    summed[...] = total.astype(BF16)
    sums = lax.dot_general(
        lanes_of(total.shape[1]),
        total * total,
        (((1,), (1,)), ((), ())),
        precision=lax.Precision.HIGHEST,
        preferred_element_type=F32,
    )
    row = lax.broadcasted_iota(jnp.int32, sums.shape, 0)
    lane = lax.broadcasted_iota(jnp.int32, sums.shape, 1)
    squares[...] = sums + jnp.where((row == scalars[0]) & (lane >= scalars[1]), INVALID, 0.0)


def finish_kernel(scalars, kept, sent, seed, out):
    summed = kept[...].astype(F32) + sent[...].astype(F32)
    factor = lax.rsqrt(jnp.mean(summed * summed, axis=-1, keepdims=True) + 1e-06)
    result = keep_share * summed * factor + (1.0 - keep_share) * seed[...].astype(F32)
    row = lax.broadcasted_iota(jnp.int32, summed.shape, 0)
    out[...] = jnp.where(row < scalars[1], result, 0.0).astype(BF16)


def body(embeddings, labels, cluster_rows):
    rows, classes = labels.shape
    depth = embeddings.shape[1]
    groups = lax.axis_size("grp")
    steps, weight = ([1], 2.0) if groups == 2 else ([1, -1], 1.0)
    place = (lax.axis_index("dev") % QUAD).astype(jnp.int32)
    clusters = jnp.stack([place, place ^ 2, place ^ 1, place ^ 3])
    scalars = jnp.stack([place, cluster_rows[0]])
    stack = pltpu.VMEM((QUAD * rows, classes // QUAD), BF16)
    total = pltpu.VMEM((QUAD * rows, classes // QUAD), F32)
    packed = like(labels.shape, BF16)
    piece = like((rows, classes // QUAD), BF16)
    matrix = like((QUAD * rows, QUAD * rows), BF16)

    half_rows = rows // 2
    unit_half = like((half_rows, depth), BF16)

    unit, unit_a, unit_b = call(
        unit_kernel, "unit", (embeddings,), (like(embeddings.shape, BF16), unit_half, unit_half)
    )
    side_a = from_side(unit_a)
    unit_up = from_up(unit)
    seed, *pieces = call(seed_kernel, "seed", (scalars, labels), (packed, piece, piece, piece))
    received = exchange(pieces)
    unit_core = from_core(unit)
    cross_unit = [from_group(after(unit, seed), step) for step in steps]
    up_side_a = from_up(side_a)
    side_b = from_side(after(jnp.concatenate([after(unit_b, side_a), unit_up[half_rows:]]), received[1:]))
    received[0] = after(received[0], unit_up)
    packed_seed = call(pack_kernel, "pack", (scalars, seed, *received), packed)
    seed_up = from_up(packed_seed)
    seed_cross = [from_group(packed_seed, step) for step in steps]
    cross0 = call(
        functools.partial(cross_kernel, weight), "cross", (unit, *cross_unit), like((len(steps) * rows, rows), BF16)
    )
    across_a, up_core, up_across_a = from_core(side_a), from_core(unit_up), from_core(after(up_side_a, packed_seed))
    unit_stack = like((QUAD * rows, depth), BF16)
    units, up_units, seed_stack = call(
        stage_kernel,
        "stage",
        (clusters, unit, side_a, unit_core, across_a, unit_up, up_side_a, up_core, up_across_a, packed_seed),
        (unit_stack, unit_stack, like((QUAD * rows, classes // QUAD), BF16)),
    )
    side_b = after(side_b, (cross0, units))
    across_b = from_core(side_b)
    cross0 = after(cross0, (side_b, seed_up, seed_cross))
    cross1, cross2 = from_side(cross0), from_core(cross0)
    units, _, far, sums = call(
        far_kernel,
        "far",
        (clusters, units, up_units, side_b, across_b, seed_stack),
        (unit_stack, unit_stack, matrix, packed),
        aliases={1: 0, 2: 1},
    )
    near = call(near_kernel, "near", (units,), matrix)
    cross3 = from_core(after(cross1, near))

    sent = from_down(sums)
    crosses = (cross0, cross1, cross2, cross3)
    kept = call(
        gather_kernel,
        "gather",
        (clusters, near, far, *crosses, packed_seed, seed_up, *seed_cross),
        like(labels.shape, F32),
        [stack, total],
    )
    summed, squares = call(combine_kernel, "combine", (scalars, kept, sent), (packed, like((8, rows), F32)))

    summed_up = from_up(summed)
    summed_cross = [from_group(summed, step) for step in steps]
    factor, current, current_stack, sums, *pieces = call(
        mix_kernel,
        "mix",
        (scalars, far, summed, squares, *exchange([squares] * 3), packed_seed),
        (
            like((8, rows), F32), packed, like((QUAD * rows, classes // QUAD), BF16),
            packed, piece, piece, piece,
        ),
    )
    received = exchange(pieces)
    near_total = call(near_products, "near_products", (near, after(current_stack, received[0])), like((QUAD * rows, classes // QUAD), F32))
    factor = after(factor, near_total)
    factor_up = from_up(factor)
    factor_cross = [from_group(factor, step) for step in steps]
    received[0] = after(received[0], (summed_up, summed_cross, factor_up, factor_cross, near_total))
    sums = call(pack_kernel, "pack", (scalars, sums, *received), packed)
    sent = from_down(sums)
    summed_up = after(summed_up, sums)
    triples = [summed_up, factor_up, seed_up]
    for s, f, own in zip(summed_cross, factor_cross, seed_cross):
        triples += [s, f, own]
    _, kept, *pieces = call(
        gather_mixed_kernel,
        "gather_mixed",
        (clusters, far, *crosses, near_total, *triples),
        (like((QUAD * rows, classes // QUAD), F32), packed, piece, piece, piece),
        [pltpu.VMEM(labels.shape, BF16), stack],
        aliases={6: 0},
    )
    kept = call(pack_kernel, "pack", (scalars, kept, *exchange(pieces)), packed)
    return call(finish_kernel, "finish", (scalars, kept, sent, seed), packed)


def solution(mesh):
    placed = (P(("grp", "dev"), None), P(("grp", "dev"), None), P(("grp", "dev")))
    return jax.shard_map(
        body, mesh=mesh, in_specs=placed, out_specs=P(("grp", "dev"), None), check_vma=False
    )
```

```python
import functools
import math

import jax
import jax.numpy as jnp
from jax import lax
from jax.experimental import pallas as pl
from jax.experimental.pallas import tpu as pltpu
from jax.sharding import PartitionSpec as P

sharpness = 25.0
keep_share = 0.8
BF16 = jnp.bfloat16
F32 = jnp.float32
QUAD = 4
INVALID = 1e38
FACTORS = 16
MB = 2**20


def along_dev(block, source):
    size = lax.axis_size("dev")
    return lax.ppermute(block, "dev", [(source(i) % size, i) for i in range(size)])


def from_up(block):
    return along_dev(block, lambda i: i + QUAD)


def from_down(block):
    return along_dev(block, lambda i: i - QUAD)


def from_side(block):
    return along_dev(block, lambda i: i ^ 2)


def from_core(block):
    return along_dev(block, lambda i: i ^ 1)


def from_group(block, step):
    size = lax.axis_size("grp")
    return lax.ppermute(block, "grp", [((i + step) % size, i) for i in range(size)])


def after(value, earlier):
    return lax.optimization_barrier((value, earlier))[0]


def exchange(pieces):
    return [along_dev(piece, lambda i, m=m: i ^ m) for m, piece in enumerate(pieces, 1)]


def call(kernel, name, operands, out_shape, scratch=(), limit=12, aliases={}):
    specs = [
        pl.BlockSpec(memory_space=pltpu.SMEM if x.dtype == jnp.int32 else pltpu.VMEM) for x in operands
    ]
    return pl.pallas_call(
        kernel,
        in_specs=specs,
        out_shape=out_shape,
        scratch_shapes=list(scratch),
        input_output_aliases=aliases,
        compiler_params=pltpu.CompilerParams(vmem_limit_bytes=limit * MB),
        name=name,
    )(*operands)


def like(shape, dtype):
    return jax.ShapeDtypeStruct(tuple(shape), dtype)


def dot(left, right):
    return jnp.dot(left, right, preferred_element_type=F32)


def affinity(left, right):
    cosine = lax.dot_general(left, right, (((1,), (1,)), ((), ())), preferred_element_type=F32)
    return jnp.exp2(cosine * (sharpness * math.log2(math.e)))


def cut(block, place, pieces):
    quarter = block.shape[1] // QUAD
    for k in range(QUAD):
        for m, piece in pieces:

            @pl.when(place ^ m == k)
            def _():
                piece[...] = block[:, k * quarter : (k + 1) * quarter]


def join(place, pieces, out):
    quarter = out.shape[1] // QUAD
    for k in range(QUAD):
        for m, piece in pieces:

            @pl.when(place ^ m == k)
            def _():
                out[:, k * quarter : (k + 1) * quarter] = piece[...]


def unit_kernel(embeddings, unit, *parts):
    values = embeddings[...].astype(F32)
    scaled = values * lax.rsqrt(jnp.mean(values * values, axis=-1, keepdims=True) + 1e-06)
    unit[...] = (scaled / math.sqrt(values.shape[-1])).astype(BF16)
    halve(unit, parts)


def halve(block, parts):
    first = 0
    for part in parts:
        part[...] = block[first : first + part.shape[0], :]
        first = first + part.shape[0]


def seed_kernel(scalars, labels, seed, *pieces):
    row = lax.broadcasted_iota(jnp.int32, labels.shape, 0)
    seed[...] = jnp.where(row < scalars[1], labels[...].astype(F32), 0.0).astype(BF16)
    cut(seed, scalars[0], list(enumerate(pieces, 1)))


def pack_kernel(scalars, whole, p1, p2, p3, out, *parts):
    out[...] = whole[...]
    join(scalars[0], [(1, p1), (2, p2), (3, p3)], out)
    halve(out, parts)


def at(cluster, rows):
    return pl.ds(pl.multiple_of(cluster * rows, rows), rows)


def place_rows(cluster, blocks, rows, stack):
    start = cluster * rows
    for block in blocks:
        count = block.shape[0]
        stack[pl.ds(pl.multiple_of(start, count), count), :] = block[...]
        start = start + count


def near_kernel(units, near):
    rows = units.shape[0] // QUAD
    for k in range(QUAD):
        for pair in range(2):
            span = slice(2 * pair * rows, 2 * (pair + 1) * rows)
            tile = affinity(units[k * rows : (k + 1) * rows, :], units[span, :])
            if k // 2 == pair:
                row = lax.broadcasted_iota(jnp.int32, tile.shape, 0)
                lane = lax.broadcasted_iota(jnp.int32, tile.shape, 1)
                tile = jnp.where(row + (k % 2) * rows == lane, 0.0, tile)
            near[k * rows : (k + 1) * rows, span] = tile.astype(BF16)


def stage_kernel(clusters, unit, side_a, core, across_a, up, up_side_a, up_core, up_across_a, own, units, up_units, stack):
    rows = unit.shape[0]
    for i, (mine, upper) in enumerate(
        ((unit, up), (side_a, up_side_a), (core, up_core), (across_a, up_across_a))
    ):
        place_rows(clusters[i], (mine,), rows, units)
        place_rows(clusters[i], (upper,), rows, up_units)
    unpack(own, stack)


def far_kernel(clusters, units_in, up_in, side_b, across_b, stack, units, up_units, far, sums):
    rows = units.shape[0] // QUAD
    half = rows // 2
    for i, block in ((1, side_b), (3, across_b)):
        start = pl.multiple_of(clusters[i] * rows + half, half)
        units[pl.ds(start, half), :] = block[:half, :]
        up_units[pl.ds(start, half), :] = block[half:, :]
    for k in range(QUAD):
        here = slice(k * rows, (k + 1) * rows)
        for first in range(0, k + 1, 2):
            span = slice(first * rows, min(first + 2, k + 1) * rows)
            far[here, span] = affinity(units[here, :], up_units[span, :]).astype(BF16)
    scatter(far, stack, sums)


def unpack(block, stack):
    rows, quarter = stack.shape[0] // QUAD, stack.shape[1]
    for k in range(QUAD):
        stack[k * rows : (k + 1) * rows, :] = block[:, k * quarter : (k + 1) * quarter]


def scatter(far, stack, out):
    rows, quarter = stack.shape[0] // QUAD, stack.shape[1]
    for k in range(QUAD):
        total = lax.dot_general(
            far[k * rows :, k * rows : (k + 1) * rows],
            stack[k * rows :, :],
            (((0,), (0,)), ((), ())),
            preferred_element_type=F32,
        )
        out[:, k * quarter : (k + 1) * quarter] = total.astype(out.dtype)


def mix_kernel(scalars, far, summed, s0, s1, s2, s3, seed, tail, mixed, stack, out, p1, p2, p3):
    total = (s0[...] + s1[...]) + (s2[...] + s3[...])
    rows = summed.shape[0]
    kept = tail.shape[0] - 2 * FACTORS
    factor = jnp.where(total > INVALID / 10, 0.0, lax.rsqrt(total / summed.shape[1] + 1e-06))
    high = factor.astype(BF16)
    tail[:kept, :] = summed[rows - kept :, :]
    tail[kept:, :] = jnp.zeros((2 * FACTORS, tail.shape[1]), BF16)
    tail[kept : kept + FACTORS, :rows] = high
    tail[kept + FACTORS :, :rows] = (factor - high.astype(F32)).astype(BF16)
    mix(summed.at[: rows - kept], tail, seed, mixed)
    unpack(mixed, stack)
    scatter(far, stack, out)
    cut(out, scalars[0], [(1, p1), (2, p2), (3, p3)])


def cross_kernel(weight, unit, *rest):
    others, out = rest[:-1], rest[-1]
    rows = unit.shape[0]
    for n, other in enumerate(others):
        out[n * rows : (n + 1) * rows, :] = (affinity(unit[...], other[...]) * weight).astype(BF16)


def near_products(near, stack, total):
    rows = stack.shape[0] // QUAD
    for k in range(QUAD):
        here = slice(k * rows, (k + 1) * rows)
        total[here, :] = dot(near[here, :], stack[...])


def cross_products(clusters, tiles, n, stack, total):
    rows = stack.shape[0] // QUAD
    for i, tile in enumerate(tiles):
        here = at(clusters[i], rows)
        total[here, :] += dot(tile[n * rows : (n + 1) * rows, :], stack[here, :])


def far_products(far, stack, total, out):
    rows, quarter = stack.shape[0] // QUAD, stack.shape[1]
    for k in range(QUAD):
        here = slice(k * rows, (k + 1) * rows)
        done = total[here, :] + dot(far[here, : (k + 1) * rows], stack[: (k + 1) * rows, :])
        out[:, k * quarter : (k + 1) * quarter] = done.astype(out.dtype)


def gather_kernel(clusters, near, far, t0, t1, t2, t3, own, up, *rest):
    cross, (out, stack, total) = rest[:-3], rest[-3:]
    unpack(own, stack)
    near_products(near, stack, total)
    for n, block in enumerate(cross):
        unpack(block, stack)
        cross_products(clusters, (t0, t1, t2, t3), n, stack, total)
    unpack(up, stack)
    far_products(far, stack, total, out)


def gather_mixed_kernel(clusters, far, t0, t1, t2, t3, total_in, *rest):
    triples, (total, out, p1, p2, p3, mixed, stack) = rest[:-7], rest[-7:]
    triples = [triples[i : i + 3] for i in range(0, len(triples), 3)]
    for n, triple in enumerate(triples[1:]):
        mix(*triple, mixed)
        unpack(mixed, stack)
        cross_products(clusters, (t0, t1, t2, t3), n, stack, total)
    mix(*triples[0], mixed)
    unpack(mixed, stack)
    far_products(far, stack, total, out)
    cut(out, clusters[0], [(1, p1), (2, p2), (3, p3)])


def lanes_of(count, lanes):
    quarter = lanes // QUAD
    row = lax.broadcasted_iota(jnp.int32, (count, lanes), 0) & (FACTORS - 1)
    lane = lax.broadcasted_iota(jnp.int32, (count, lanes), 1)
    return ((lane >= row * quarter) & (lane < (row + 1) * quarter)).astype(F32).astype(BF16)


def mix(head, tail, seed, out):
    rows, lanes = seed.shape
    first = head.shape[0]
    kept = rows - first
    spread = lax.dot_general(
        tail[kept:, :rows],
        lanes_of(2 * FACTORS, lanes),
        (((0,), (0,)), ((), ())),
        preferred_element_type=F32,
    )
    for block, start, stop in ((head[...], 0, first), (tail[:kept, :], first, rows)):
        share = keep_share * block.astype(F32) * spread[start:stop, :]
        out[start:stop, :] = (share + (1.0 - keep_share) * seed[start:stop, :].astype(F32)).astype(BF16)


def combine_kernel(scalars, kept, sent, summed, head, squares):
    total = kept[...] + sent[...].astype(F32)
    summed[...] = total.astype(BF16)
    head[...] = summed[: head.shape[0], :]
    square = total * total
    high = square.astype(BF16)
    marks = lanes_of(FACTORS, total.shape[1])
    sums = sum(
        lax.dot_general(marks, part, (((1,), (1,)), ((), ())), preferred_element_type=F32)
        for part in (high, (square - high.astype(F32)).astype(BF16))
    )
    row = lax.broadcasted_iota(jnp.int32, sums.shape, 0)
    lane = lax.broadcasted_iota(jnp.int32, sums.shape, 1)
    squares[...] = sums + jnp.where((row == scalars[0]) & (lane >= scalars[1]), INVALID, 0.0)


def finish_kernel(scalars, kept, sent, seed, out):
    summed = kept[...].astype(F32) + sent[...].astype(F32)
    factor = lax.rsqrt(jnp.mean(summed * summed, axis=-1, keepdims=True) + 1e-06)
    result = keep_share * summed * factor + (1.0 - keep_share) * seed[...].astype(F32)
    row = lax.broadcasted_iota(jnp.int32, summed.shape, 0)
    out[...] = jnp.where(row < scalars[1], result, 0.0).astype(BF16)


def body(embeddings, labels, cluster_rows):
    rows, classes = labels.shape
    depth = embeddings.shape[1]
    groups = lax.axis_size("grp")
    steps, weight = ([1], 2.0) if groups == 2 else ([1, -1], 1.0)
    place = (lax.axis_index("dev") % QUAD).astype(jnp.int32)
    clusters = jnp.stack([place, place ^ 2, place ^ 1, place ^ 3])
    scalars = jnp.stack([place, cluster_rows[0]])
    stack = pltpu.VMEM((QUAD * rows, classes // QUAD), BF16)
    total = pltpu.VMEM((QUAD * rows, classes // QUAD), F32)
    packed = like(labels.shape, BF16)
    piece = like((rows, classes // QUAD), BF16)
    matrix = like((QUAD * rows, QUAD * rows), BF16)

    half_rows = rows // 2
    unit_half = like((half_rows, depth), BF16)

    unit, unit_a, unit_b = call(
        unit_kernel, "unit", (embeddings,), (like(embeddings.shape, BF16), unit_half, unit_half)
    )
    side_a = from_side(unit_a)
    unit_up = from_up(unit)
    seed, *pieces = call(seed_kernel, "seed", (scalars, labels), (packed, piece, piece, piece))
    received = exchange(pieces)
    unit_core = from_core(unit)
    cross_unit = [from_group(after(unit, seed), step) for step in steps]
    up_side_a = from_up(side_a)
    side_b = from_side(after(jnp.concatenate([after(unit_b, side_a), unit_up[half_rows:]]), received[1:]))
    received[0] = after(received[0], unit_up)
    packed_seed = call(pack_kernel, "pack", (scalars, seed, *received), packed)
    seed_up = from_up(packed_seed)
    seed_cross = [from_group(packed_seed, step) for step in steps]
    cross0 = call(
        functools.partial(cross_kernel, weight), "cross", (unit, *cross_unit), like((len(steps) * rows, rows), BF16)
    )
    side_b = after(side_b, (packed_seed, cross0, up_side_a))
    across_b = from_core(side_b)
    across_a, up_core, up_across_a = from_core(side_a), from_core(unit_up), from_core(up_side_a)
    unit_stack = like((QUAD * rows, depth), BF16)
    units, up_units, seed_stack = call(
        stage_kernel,
        "stage",
        (
            clusters, after(unit, side_b), side_a, unit_core, across_a, unit_up, up_side_a, up_core, up_across_a,
            packed_seed,
        ),
        (unit_stack, unit_stack, like((QUAD * rows, classes // QUAD), BF16)),
    )
    cross0 = after(cross0, (side_b, seed_up, seed_cross))
    cross1, cross2 = from_side(cross0), from_core(cross0)
    units, _, far, sums = call(
        far_kernel,
        "far",
        (clusters, units, up_units, side_b, across_b, seed_stack),
        (unit_stack, unit_stack, matrix, packed),
        aliases={1: 0, 2: 1},
    )
    near = call(near_kernel, "near", (units,), matrix)
    cross3 = from_core(after(cross1, near))

    sent = from_down(sums)
    crosses = (cross0, cross1, cross2, cross3)
    kept = call(
        gather_kernel,
        "gather",
        (clusters, near, far, *crosses, packed_seed, seed_up, *seed_cross),
        like(labels.shape, F32),
        [stack, total],
    )
    tail_rows = rows // 96 * 16
    head = like((rows - tail_rows, classes), BF16)
    tail = like((tail_rows + 2 * FACTORS, classes), BF16)
    summed, head, squares = call(
        combine_kernel, "combine", (scalars, kept, sent), (packed, head, like((FACTORS, rows), F32))
    )

    head_up = from_up(head)
    head_cross = [from_group(head, step) for step in steps]
    tail, current, current_stack, sums, *pieces = call(
        mix_kernel,
        "mix",
        (scalars, far, summed, squares, *exchange([squares] * 3), packed_seed),
        (tail, packed, like((QUAD * rows, classes // QUAD), BF16), packed, piece, piece, piece),
    )
    received = exchange(pieces)
    near_total = call(
        near_products,
        "near_products",
        (near, after(current_stack, received[0])),
        like((QUAD * rows, classes // QUAD), F32),
    )
    tail = after(tail, near_total)
    tail_up = from_up(tail)
    tail_cross = [from_group(tail, step) for step in steps]
    sums = call(pack_kernel, "pack", (scalars, sums, *received), packed)
    sums = after(sums, (head_up, head_cross, tail_up, tail_cross))
    sent = from_down(sums)
    head_up = after(head_up, sums)
    triples = [head_up, tail_up, seed_up]
    for top, rest, own in zip(head_cross, tail_cross, seed_cross):
        triples += [top, rest, own]
    _, kept, *pieces = call(
        gather_mixed_kernel,
        "gather_mixed",
        (clusters, far, *crosses, near_total, *triples),
        (like((QUAD * rows, classes // QUAD), F32), packed, piece, piece, piece),
        [pltpu.VMEM(labels.shape, BF16), stack],
        aliases={6: 0},
    )
    kept = call(pack_kernel, "pack", (scalars, kept, *exchange(pieces)), packed)
    return call(finish_kernel, "finish", (scalars, kept, sent, seed), packed)


def solution(mesh):
    placed = (P(("grp", "dev"), None), P(("grp", "dev"), None), P(("grp", "dev")))
    return jax.shard_map(
        body, mesh=mesh, in_specs=placed, out_specs=P(("grp", "dev"), None), check_vma=False
    )
```

```python
import functools
import math

import jax
import jax.numpy as jnp
from jax import lax
from jax.experimental import pallas as pl
from jax.experimental.pallas import tpu as pltpu
from jax.sharding import PartitionSpec as P

sharpness = 25.0
keep_share = 0.8
BF16 = jnp.bfloat16
F32 = jnp.float32
QUAD = 4
INVALID = 1e38
FACTORS = 16
MB = 2**20


def along_dev(block, source):
    size = lax.axis_size("dev")
    return lax.ppermute(block, "dev", [(source(i) % size, i) for i in range(size)])


def from_up(block):
    return along_dev(block, lambda i: i + QUAD)


def from_down(block):
    return along_dev(block, lambda i: i - QUAD)


def from_side(block):
    return along_dev(block, lambda i: i ^ 2)


def from_core(block):
    return along_dev(block, lambda i: i ^ 1)


def from_group(block, step):
    size = lax.axis_size("grp")
    return lax.ppermute(block, "grp", [((i + step) % size, i) for i in range(size)])


def after(value, earlier):
    return lax.optimization_barrier((value, earlier))[0]


def exchange(pieces):
    return [along_dev(piece, lambda i, m=m: i ^ m) for m, piece in enumerate(pieces, 1)]


def call(kernel, name, operands, out_shape, scratch=(), limit=12, aliases={}):
    specs = [
        pl.BlockSpec(memory_space=pltpu.SMEM if x.dtype == jnp.int32 else pltpu.VMEM) for x in operands
    ]
    return pl.pallas_call(
        kernel,
        in_specs=specs,
        out_shape=out_shape,
        scratch_shapes=list(scratch),
        input_output_aliases=aliases,
        compiler_params=pltpu.CompilerParams(vmem_limit_bytes=limit * MB),
        name=name,
    )(*operands)


def like(shape, dtype):
    return jax.ShapeDtypeStruct(tuple(shape), dtype)


def dot(left, right):
    return jnp.dot(left, right, preferred_element_type=F32)


def affinity(left, right):
    cosine = lax.dot_general(left, right, (((1,), (1,)), ((), ())), preferred_element_type=F32)
    return jnp.exp2(cosine * (sharpness * math.log2(math.e)))


def cut(block, place, pieces):
    quarter = block.shape[1] // QUAD
    for k in range(QUAD):
        for m, piece in pieces:

            @pl.when(place ^ m == k)
            def _():
                piece[...] = block[:, k * quarter : (k + 1) * quarter]


def join(place, pieces, out):
    quarter = out.shape[1] // QUAD
    for k in range(QUAD):
        for m, piece in pieces:

            @pl.when(place ^ m == k)
            def _():
                out[:, k * quarter : (k + 1) * quarter] = piece[...]


def unit_rows(embeddings):
    values = embeddings.astype(F32)
    scaled = values * lax.rsqrt(jnp.mean(values * values, axis=-1, keepdims=True) + 1e-06)
    return (scaled / math.sqrt(values.shape[-1])).astype(BF16)


def seed_kernel(scalars, labels, seed, *pieces):
    row = lax.broadcasted_iota(jnp.int32, labels.shape, 0)
    seed[...] = jnp.where(row < scalars[1], labels[...].astype(F32), 0.0).astype(BF16)
    cut(seed, scalars[0], list(enumerate(pieces, 1)))


def pack_kernel(scalars, whole, p1, p2, p3, out):
    out[...] = whole[...]
    join(scalars[0], [(1, p1), (2, p2), (3, p3)], out)


def at(cluster, rows):
    return pl.ds(pl.multiple_of(cluster * rows, rows), rows)


def place_units(start, block, stack):
    count = block.shape[0]
    stack[pl.ds(pl.multiple_of(start, count), count), :] = unit_rows(block[...])


def near_kernel(units, near):
    rows = units.shape[0] // QUAD
    for k in range(QUAD):
        for pair in range(2):
            span = slice(2 * pair * rows, 2 * (pair + 1) * rows)
            tile = affinity(units[k * rows : (k + 1) * rows, :], units[span, :])
            if k // 2 == pair:
                row = lax.broadcasted_iota(jnp.int32, tile.shape, 0)
                lane = lax.broadcasted_iota(jnp.int32, tile.shape, 1)
                tile = jnp.where(row + (k % 2) * rows == lane, 0.0, tile)
            near[k * rows : (k + 1) * rows, span] = tile.astype(BF16)


def stage_kernel(clusters, own, side_a, core, across_a, units):
    rows = own.shape[0]
    for i, block in enumerate((own, side_a, core, across_a)):
        place_units(clusters[i] * rows, block, units)


def stage_seed_kernel(clusters, own, side_a, core, across_a, seed, units, stack):
    stage_kernel(clusters, own, side_a, core, across_a, units)
    unpack(seed, stack)


def far_kernel(clusters, units_in, up_in, side_b, across_b, stack, units, up_units, far, sums):
    rows = units.shape[0] // QUAD
    half = rows // 2
    for i, block in ((1, side_b), (3, across_b)):
        start = clusters[i] * rows + half
        place_units(start, block.at[:half], units)
        place_units(start, block.at[half:], up_units)
    for k in range(QUAD):
        here = slice(k * rows, (k + 1) * rows)
        for first in range(0, k + 1, 2):
            span = slice(first * rows, min(first + 2, k + 1) * rows)
            far[here, span] = affinity(units[here, :], up_units[span, :]).astype(BF16)
    scatter(far, stack, sums)


def unpack(block, stack):
    rows, quarter = stack.shape[0] // QUAD, stack.shape[1]
    for k in range(QUAD):
        stack[k * rows : (k + 1) * rows, :] = block[:, k * quarter : (k + 1) * quarter]


def scatter(far, stack, out):
    rows, quarter = stack.shape[0] // QUAD, stack.shape[1]
    for k in range(QUAD):
        total = lax.dot_general(
            far[k * rows :, k * rows : (k + 1) * rows],
            stack[k * rows :, :],
            (((0,), (0,)), ((), ())),
            preferred_element_type=F32,
        )
        out[:, k * quarter : (k + 1) * quarter] = total.astype(out.dtype)


def mix_kernel(scalars, far, summed, s0, s1, s2, s3, seed, tail, mixed, stack, out, p1, p2, p3):
    total = (s0[...] + s1[...]) + (s2[...] + s3[...])
    rows = summed.shape[0]
    kept = tail.shape[0] - 2 * FACTORS
    factor = jnp.where(total > INVALID / 10, 0.0, lax.rsqrt(total / summed.shape[1] + 1e-06))
    high = factor.astype(BF16)
    tail[:kept, :] = summed[rows - kept :, :]
    tail[kept:, :] = jnp.zeros((2 * FACTORS, tail.shape[1]), BF16)
    tail[kept : kept + FACTORS, :rows] = high
    tail[kept + FACTORS :, :rows] = (factor - high.astype(F32)).astype(BF16)
    mix(summed.at[: rows - kept], tail, seed, mixed)
    unpack(mixed, stack)
    scatter(far, stack, out)
    cut(out, scalars[0], [(1, p1), (2, p2), (3, p3)])


def cross_kernel(weight, own, *rest):
    others, out = rest[:-1], rest[-1]
    rows = own.shape[0]
    unit = unit_rows(own[...])
    for n, other in enumerate(others):
        out[n * rows : (n + 1) * rows, :] = (affinity(unit, unit_rows(other[...])) * weight).astype(BF16)


def near_products(near, stack, total):
    rows = stack.shape[0] // QUAD
    for k in range(QUAD):
        here = slice(k * rows, (k + 1) * rows)
        total[here, :] = dot(near[here, :], stack[...])


def cross_products(clusters, tiles, n, stack, total):
    rows = stack.shape[0] // QUAD
    for i, tile in enumerate(tiles):
        here = at(clusters[i], rows)
        total[here, :] += dot(tile[n * rows : (n + 1) * rows, :], stack[here, :])


def far_products(far, stack, total, out):
    rows, quarter = stack.shape[0] // QUAD, stack.shape[1]
    for k in range(QUAD):
        here = slice(k * rows, (k + 1) * rows)
        done = total[here, :] + dot(far[here, : (k + 1) * rows], stack[: (k + 1) * rows, :])
        out[:, k * quarter : (k + 1) * quarter] = done.astype(out.dtype)


def gather_kernel(clusters, near, far, t0, t1, t2, t3, own, up, *rest):
    cross, (out, stack, total) = rest[:-3], rest[-3:]
    unpack(own, stack)
    near_products(near, stack, total)
    for n, block in enumerate(cross):
        unpack(block, stack)
        cross_products(clusters, (t0, t1, t2, t3), n, stack, total)
    unpack(up, stack)
    far_products(far, stack, total, out)


def gather_mixed_kernel(clusters, far, t0, t1, t2, t3, total_in, *rest):
    triples, (total, out, p1, p2, p3, mixed, stack) = rest[:-7], rest[-7:]
    triples = [triples[i : i + 3] for i in range(0, len(triples), 3)]
    for n, triple in enumerate(triples[1:]):
        mix(*triple, mixed)
        unpack(mixed, stack)
        cross_products(clusters, (t0, t1, t2, t3), n, stack, total)
    mix(*triples[0], mixed)
    unpack(mixed, stack)
    far_products(far, stack, total, out)
    cut(out, clusters[0], [(1, p1), (2, p2), (3, p3)])


def lanes_of(count, lanes):
    quarter = lanes // QUAD
    row = lax.broadcasted_iota(jnp.int32, (count, lanes), 0) & (FACTORS - 1)
    lane = lax.broadcasted_iota(jnp.int32, (count, lanes), 1)
    return ((lane >= row * quarter) & (lane < (row + 1) * quarter)).astype(F32).astype(BF16)


def mix(head, tail, seed, out):
    rows, lanes = seed.shape
    first = head.shape[0]
    kept = rows - first
    spread = lax.dot_general(
        tail[kept:, :rows],
        lanes_of(2 * FACTORS, lanes),
        (((0,), (0,)), ((), ())),
        preferred_element_type=F32,
    )
    for block, start, stop in ((head[...], 0, first), (tail[:kept, :], first, rows)):
        share = keep_share * block.astype(F32) * spread[start:stop, :]
        out[start:stop, :] = (share + (1.0 - keep_share) * seed[start:stop, :].astype(F32)).astype(BF16)


def combine_kernel(scalars, kept, sent, summed, head, squares):
    total = kept[...] + sent[...].astype(F32)
    summed[...] = total.astype(BF16)
    head[...] = summed[: head.shape[0], :]
    square = total * total
    high = square.astype(BF16)
    marks = lanes_of(FACTORS, total.shape[1])
    sums = sum(
        lax.dot_general(marks, part, (((1,), (1,)), ((), ())), preferred_element_type=F32)
        for part in (high, (square - high.astype(F32)).astype(BF16))
    )
    row = lax.broadcasted_iota(jnp.int32, sums.shape, 0)
    lane = lax.broadcasted_iota(jnp.int32, sums.shape, 1)
    squares[...] = sums + jnp.where((row == scalars[0]) & (lane >= scalars[1]), INVALID, 0.0)


def finish_kernel(scalars, kept, sent, seed, out):
    summed = kept[...].astype(F32) + sent[...].astype(F32)
    factor = lax.rsqrt(jnp.mean(summed * summed, axis=-1, keepdims=True) + 1e-06)
    result = keep_share * summed * factor + (1.0 - keep_share) * seed[...].astype(F32)
    row = lax.broadcasted_iota(jnp.int32, summed.shape, 0)
    out[...] = jnp.where(row < scalars[1], result, 0.0).astype(BF16)


def body(embeddings, labels, cluster_rows):
    rows, classes = labels.shape
    depth = embeddings.shape[1]
    groups = lax.axis_size("grp")
    steps, weight = ([1], 2.0) if groups == 2 else ([1, -1], 1.0)
    place = (lax.axis_index("dev") % QUAD).astype(jnp.int32)
    clusters = jnp.stack([place, place ^ 2, place ^ 1, place ^ 3])
    scalars = jnp.stack([place, cluster_rows[0]])
    stack = pltpu.VMEM((QUAD * rows, classes // QUAD), BF16)
    total = pltpu.VMEM((QUAD * rows, classes // QUAD), F32)
    packed = like(labels.shape, BF16)
    piece = like((rows, classes // QUAD), BF16)
    matrix = like((QUAD * rows, QUAD * rows), BF16)

    half_rows = rows // 2

    own_up = from_up(embeddings)
    side_a = from_side(embeddings[:half_rows])
    seed, *pieces = call(seed_kernel, "seed", (scalars, labels), (packed, piece, piece, piece))
    received = exchange(pieces)
    own_core = from_core(embeddings)
    cross_own = [from_group(after(embeddings, seed), step) for step in steps]
    up_side_a = from_up(side_a)
    late = jnp.concatenate([after(embeddings, side_a)[half_rows:], own_up[half_rows:]])
    side_b = from_side(after(late, received[1:]))
    received[0] = after(received[0], own_up)
    packed_seed = call(pack_kernel, "pack", (scalars, seed, *received), packed)
    seed_up = from_up(packed_seed)
    seed_cross = [from_group(packed_seed, step) for step in steps]
    cross0 = call(
        functools.partial(cross_kernel, weight), "cross", (embeddings, *cross_own), like((len(steps) * rows, rows), BF16)
    )
    across_a = from_core(side_a)
    unit_stack = like((QUAD * rows, depth), BF16)
    units, seed_stack = call(
        stage_seed_kernel,
        "stage_own",
        (clusters, embeddings, side_a, own_core, across_a, packed_seed),
        (unit_stack, like((QUAD * rows, classes // QUAD), BF16)),
    )
    side_b = after(side_b, (cross0, units, up_side_a))
    across_b = from_core(side_b)
    up_core, up_across_a = from_core(own_up), from_core(up_side_a)
    up_units = call(
        stage_kernel, "stage_up", (clusters, after(own_up, side_b), up_side_a, up_core, up_across_a), unit_stack
    )
    cross0 = after(cross0, (side_b, seed_up, seed_cross))
    cross1, cross2 = from_side(cross0), from_core(cross0)
    units, _, far, sums = call(
        far_kernel,
        "far",
        (clusters, units, up_units, side_b, across_b, seed_stack),
        (unit_stack, unit_stack, matrix, packed),
        aliases={1: 0, 2: 1},
    )
    near = call(near_kernel, "near", (units,), matrix)
    cross3 = from_core(after(cross1, near))

    sent = from_down(sums)
    crosses = (cross0, cross1, cross2, cross3)
    kept = call(
        gather_kernel,
        "gather",
        (clusters, near, far, *crosses, packed_seed, seed_up, *seed_cross),
        like(labels.shape, F32),
        [stack, total],
    )
    tail_rows = rows // 96 * 16
    head = like((rows - tail_rows, classes), BF16)
    tail = like((tail_rows + 2 * FACTORS, classes), BF16)
    summed, head, squares = call(
        combine_kernel, "combine", (scalars, kept, sent), (packed, head, like((FACTORS, rows), F32))
    )

    head_up = from_up(head)
    head_cross = [from_group(head, step) for step in steps]
    tail, current, current_stack, sums, *pieces = call(
        mix_kernel,
        "mix",
        (scalars, far, summed, squares, *exchange([squares] * 3), packed_seed),
        (tail, packed, like((QUAD * rows, classes // QUAD), BF16), packed, piece, piece, piece),
    )
    received = exchange(pieces)
    near_total = call(
        near_products,
        "near_products",
        (near, after(current_stack, received[0])),
        like((QUAD * rows, classes // QUAD), F32),
    )
    tail = after(tail, near_total)
    tail_up = from_up(tail)
    tail_cross = [from_group(tail, step) for step in steps]
    sums = call(pack_kernel, "pack", (scalars, sums, *received), packed)
    sums = after(sums, (head_up, head_cross, tail_up, tail_cross))
    sent = from_down(sums)
    head_up = after(head_up, sums)
    triples = [head_up, tail_up, seed_up]
    for top, rest, own in zip(head_cross, tail_cross, seed_cross):
        triples += [top, rest, own]
    _, kept, *pieces = call(
        gather_mixed_kernel,
        "gather_mixed",
        (clusters, far, *crosses, near_total, *triples),
        (like((QUAD * rows, classes // QUAD), F32), packed, piece, piece, piece),
        [pltpu.VMEM(labels.shape, BF16), stack],
        aliases={6: 0},
    )
    kept = call(pack_kernel, "pack", (scalars, kept, *exchange(pieces)), packed)
    return call(finish_kernel, "finish", (scalars, kept, sent, seed), packed)


def solution(mesh):
    placed = (P(("grp", "dev"), None), P(("grp", "dev"), None), P(("grp", "dev")))
    return jax.shard_map(
        body, mesh=mesh, in_specs=placed, out_specs=P(("grp", "dev"), None), check_vma=False
    )
```

```python
import functools
import math

import jax
import jax.numpy as jnp
from jax import lax
from jax.experimental import pallas as pl
from jax.experimental.pallas import tpu as pltpu
from jax.sharding import PartitionSpec as P

sharpness = 25.0
keep_share = 0.8
BF16 = jnp.bfloat16
F32 = jnp.float32
QUAD = 4
INVALID = 1e38
FACTORS = 16
MB = 2**20


def along_dev(block, source):
    size = lax.axis_size("dev")
    return lax.ppermute(block, "dev", [(source(i) % size, i) for i in range(size)])


def from_up(block):
    return along_dev(block, lambda i: i + QUAD)


def from_down(block):
    return along_dev(block, lambda i: i - QUAD)


def from_side(block):
    return along_dev(block, lambda i: i ^ 2)


def from_core(block):
    return along_dev(block, lambda i: i ^ 1)


def from_group(block, step):
    size = lax.axis_size("grp")
    return lax.ppermute(block, "grp", [((i + step) % size, i) for i in range(size)])


def after(value, earlier):
    return lax.optimization_barrier((value, earlier))[0]


def exchange(pieces):
    return [along_dev(piece, lambda i, m=m: i ^ m) for m, piece in enumerate(pieces, 1)]


def call(kernel, name, operands, out_shape, scratch=(), limit=12, aliases={}):
    specs = [
        pl.BlockSpec(memory_space=pltpu.SMEM if x.dtype == jnp.int32 else pltpu.VMEM) for x in operands
    ]
    return pl.pallas_call(
        kernel,
        in_specs=specs,
        out_shape=out_shape,
        scratch_shapes=list(scratch),
        input_output_aliases=aliases,
        compiler_params=pltpu.CompilerParams(vmem_limit_bytes=limit * MB),
        name=name,
    )(*operands)


def like(shape, dtype):
    return jax.ShapeDtypeStruct(tuple(shape), dtype)


def dot(left, right):
    return jnp.dot(left, right, preferred_element_type=F32)


def affinity(left, right):
    cosine = lax.dot_general(left, right, (((1,), (1,)), ((), ())), preferred_element_type=F32)
    return jnp.exp2(cosine * (sharpness * math.log2(math.e)))


def cut(block, place, pieces):
    quarter = block.shape[1] // QUAD
    for k in range(QUAD):
        for m, piece in pieces:

            @pl.when(place ^ m == k)
            def _():
                piece[...] = block[:, k * quarter : (k + 1) * quarter]


def join(place, pieces, out):
    quarter = out.shape[1] // QUAD
    for k in range(QUAD):
        for m, piece in pieces:

            @pl.when(place ^ m == k)
            def _():
                out[:, k * quarter : (k + 1) * quarter] = piece[...]


def unit_rows(embeddings):
    values = embeddings.astype(F32)
    scaled = values * lax.rsqrt(jnp.mean(values * values, axis=-1, keepdims=True) + 1e-06)
    return (scaled / math.sqrt(values.shape[-1])).astype(BF16)


def seed_kernel(scalars, labels, seed, *pieces):
    row = lax.broadcasted_iota(jnp.int32, labels.shape, 0)
    seed[...] = jnp.where(row < scalars[1], labels[...].astype(F32), 0.0).astype(BF16)
    cut(seed, scalars[0], list(enumerate(pieces, 1)))


def pack_kernel(scalars, whole, p1, p2, p3, out):
    out[...] = whole[...]
    join(scalars[0], [(1, p1), (2, p2), (3, p3)], out)


def at(cluster, rows):
    return pl.ds(pl.multiple_of(cluster * rows, rows), rows)


def place_units(start, block, stack):
    count = block.shape[0]
    stack[pl.ds(pl.multiple_of(start, count), count), :] = unit_rows(block[...])


def near_kernel(units, near):
    rows = units.shape[0] // QUAD
    for k in range(QUAD):
        for pair in range(2):
            span = slice(2 * pair * rows, 2 * (pair + 1) * rows)
            tile = affinity(units[k * rows : (k + 1) * rows, :], units[span, :])
            if k // 2 == pair:
                row = lax.broadcasted_iota(jnp.int32, tile.shape, 0)
                lane = lax.broadcasted_iota(jnp.int32, tile.shape, 1)
                tile = jnp.where(row + (k % 2) * rows == lane, 0.0, tile)
            near[k * rows : (k + 1) * rows, span] = tile.astype(BF16)


def stage_kernel(clusters, own, side_a, core, across_a, units):
    rows = own.shape[0]
    for i, block in enumerate((own, side_a, core, across_a)):
        place_units(clusters[i] * rows, block, units)


def stage_seed_kernel(clusters, own, side_a, core, across_a, seed, units, stack):
    stage_kernel(clusters, own, side_a, core, across_a, units)
    unpack(seed, stack)


def far_kernel(clusters, units_in, up_in, side_b, across_b, stack, units, up_units, far, sums):
    rows = units.shape[0] // QUAD
    half = rows // 2
    for i, block in ((1, side_b), (3, across_b)):
        start = clusters[i] * rows + half
        place_units(start, block.at[:half], units)
        place_units(start, block.at[half:], up_units)
    for k in range(QUAD):
        here = slice(k * rows, (k + 1) * rows)
        for first in range(0, k + 1, 2):
            span = slice(first * rows, min(first + 2, k + 1) * rows)
            far[here, span] = affinity(units[here, :], up_units[span, :]).astype(BF16)
    scatter(far, stack, (sums,))


def unpack(block, stack):
    rows, quarter = stack.shape[0] // QUAD, stack.shape[1]
    for k in range(QUAD):
        stack[k * rows : (k + 1) * rows, :] = block[:, k * quarter : (k + 1) * quarter]


def scatter(far, stack, outs):
    rows, quarter = stack.shape[0] // QUAD, stack.shape[1]
    for k in range(QUAD):
        total = lax.dot_general(
            far[k * rows :, k * rows : (k + 1) * rows],
            stack[k * rows :, :],
            (((0,), (0,)), ((), ())),
            preferred_element_type=F32,
        )
        first = 0
        for out in outs:
            out[:, k * quarter : (k + 1) * quarter] = total[first : first + out.shape[0], :].astype(out.dtype)
            first = first + out.shape[0]


def mix_kernel(scalars, far, summed, s0, s1, s2, s3, seed, tail, mixed, stack, out_b, out_a, p1, p2, p3):
    total = (s0[...] + s1[...]) + (s2[...] + s3[...])
    rows = summed.shape[0]
    kept = tail.shape[0] - 2 * FACTORS
    factor = jnp.where(total > INVALID / 10, 0.0, lax.rsqrt(total / summed.shape[1] + 1e-06))
    high = factor.astype(BF16)
    tail[:kept, :] = summed[rows - kept :, :]
    tail[kept:, :] = jnp.zeros((2 * FACTORS, tail.shape[1]), BF16)
    tail[kept : kept + FACTORS, :rows] = high
    tail[kept + FACTORS :, :rows] = (factor - high.astype(F32)).astype(BF16)
    mix(summed.at[: rows - kept], tail, seed, mixed)
    unpack(mixed, stack)
    scatter(far, stack, (out_a, out_b))
    cut(out_a, scalars[0], [(1, p1), (2, p2), (3, p3)])


def cross_kernel(weight, own, *rest):
    others, out = rest[:-1], rest[-1]
    rows = own.shape[0]
    unit = unit_rows(own[...])
    for n, other in enumerate(others):
        out[n * rows : (n + 1) * rows, :] = (affinity(unit, unit_rows(other[...])) * weight).astype(BF16)


def near_products(near, stack, total):
    rows = stack.shape[0] // QUAD
    for k in range(QUAD):
        here = slice(k * rows, (k + 1) * rows)
        total[here, :] = dot(near[here, :], stack[...])


def cross_products(clusters, tiles, n, stack, total):
    rows = stack.shape[0] // QUAD
    for i, tile in enumerate(tiles):
        here = at(clusters[i], rows)
        total[here, :] += dot(tile[n * rows : (n + 1) * rows, :], stack[here, :])


def far_products(far, stack, total, outs):
    rows, quarter = stack.shape[0] // QUAD, stack.shape[1]
    for k in range(QUAD):
        here = slice(k * rows, (k + 1) * rows)
        done = total[here, :] + dot(far[here, : (k + 1) * rows], stack[: (k + 1) * rows, :])
        first = 0
        for out in outs:
            out[:, k * quarter : (k + 1) * quarter] = done[first : first + out.shape[0], :].astype(out.dtype)
            first = first + out.shape[0]


def gather_kernel(clusters, near, far, t0, t1, t2, t3, own, up, *rest):
    cross, (out, stack, total) = rest[:-3], rest[-3:]
    unpack(own, stack)
    near_products(near, stack, total)
    for n, block in enumerate(cross):
        unpack(block, stack)
        cross_products(clusters, (t0, t1, t2, t3), n, stack, total)
    unpack(up, stack)
    far_products(far, stack, total, (out,))


def gather_mixed_kernel(clusters, far, t0, t1, t2, t3, total_in, *rest):
    triples, (total, out_b, out_a, p1, p2, p3, mixed, stack) = rest[:-8], rest[-8:]
    triples = [triples[i : i + 3] for i in range(0, len(triples), 3)]
    for n, triple in enumerate(triples[1:]):
        mix(*triple, mixed)
        unpack(mixed, stack)
        cross_products(clusters, (t0, t1, t2, t3), n, stack, total)
    mix(*triples[0], mixed)
    unpack(mixed, stack)
    far_products(far, stack, total, (out_a, out_b))
    cut(out_a, clusters[0], [(1, p1), (2, p2), (3, p3)])


def lanes_of(count, lanes):
    quarter = lanes // QUAD
    row = lax.broadcasted_iota(jnp.int32, (count, lanes), 0) & (FACTORS - 1)
    lane = lax.broadcasted_iota(jnp.int32, (count, lanes), 1)
    return ((lane >= row * quarter) & (lane < (row + 1) * quarter)).astype(F32).astype(BF16)


def mix(head, tail, seed, out):
    rows, lanes = seed.shape
    first = head.shape[0]
    kept = rows - first
    spread = lax.dot_general(
        tail[kept:, :rows],
        lanes_of(2 * FACTORS, lanes),
        (((0,), (0,)), ((), ())),
        preferred_element_type=F32,
    )
    for block, start, stop in ((head[...], 0, first), (tail[:kept, :], first, rows)):
        share = keep_share * block.astype(F32) * spread[start:stop, :]
        out[start:stop, :] = (share + (1.0 - keep_share) * seed[start:stop, :].astype(F32)).astype(BF16)


def combine_kernel(scalars, kept, sent, summed, head, squares):
    total = kept[...] + sent[...].astype(F32)
    summed[...] = total.astype(BF16)
    head[...] = summed[: head.shape[0], :]
    square = total * total
    high = square.astype(BF16)
    marks = lanes_of(FACTORS, total.shape[1])
    sums = sum(
        lax.dot_general(marks, part, (((1,), (1,)), ((), ())), preferred_element_type=F32)
        for part in (high, (square - high.astype(F32)).astype(BF16))
    )
    row = lax.broadcasted_iota(jnp.int32, sums.shape, 0)
    lane = lax.broadcasted_iota(jnp.int32, sums.shape, 1)
    squares[...] = sums + jnp.where((row == scalars[0]) & (lane >= scalars[1]), INVALID, 0.0)


def add_kernel(scalars, kept, sent, out, p1, p2, p3):
    out[...] = (kept[...] + sent[...].astype(F32)).astype(BF16)
    cut(out, scalars[0], [(1, p1), (2, p2), (3, p3)])


def finish_kernel(scalars, kept_a, sent_a, sums_b, p1, p2, p3, seed, out, whole_b):
    whole_b[...] = sums_b[...]
    join(scalars[0], [(1, p1), (2, p2), (3, p3)], whole_b)
    half = kept_a.shape[0]
    for first, summed in (
        (0, kept_a[...].astype(F32) + sent_a[...].astype(F32)),
        (half, whole_b[...].astype(F32)),
    ):
        here = slice(first, first + summed.shape[0])
        factor = lax.rsqrt(jnp.mean(summed * summed, axis=-1, keepdims=True) + 1e-06)
        result = keep_share * summed * factor + (1.0 - keep_share) * seed[here, :].astype(F32)
        row = lax.broadcasted_iota(jnp.int32, summed.shape, 0) + first
        out[here, :] = jnp.where(row < scalars[1], result, 0.0).astype(BF16)


def body(embeddings, labels, cluster_rows):
    rows, classes = labels.shape
    depth = embeddings.shape[1]
    groups = lax.axis_size("grp")
    steps, weight = ([1], 2.0) if groups == 2 else ([1, -1], 1.0)
    place = (lax.axis_index("dev") % QUAD).astype(jnp.int32)
    clusters = jnp.stack([place, place ^ 2, place ^ 1, place ^ 3])
    scalars = jnp.stack([place, cluster_rows[0]])
    stack = pltpu.VMEM((QUAD * rows, classes // QUAD), BF16)
    total = pltpu.VMEM((QUAD * rows, classes // QUAD), F32)
    packed = like(labels.shape, BF16)
    piece = like((rows, classes // QUAD), BF16)
    matrix = like((QUAD * rows, QUAD * rows), BF16)

    half_rows = rows // 2

    own_up = from_up(embeddings)
    side_a = from_side(embeddings[:half_rows])
    seed, *pieces = call(seed_kernel, "seed", (scalars, labels), (packed, piece, piece, piece))
    received = exchange(pieces)
    own_core = from_core(embeddings)
    cross_own = [from_group(after(embeddings, seed), step) for step in steps]
    up_side_a = from_up(side_a)
    late = jnp.concatenate([after(embeddings, side_a)[half_rows:], own_up[half_rows:]])
    side_b = from_side(after(late, received[1:]))
    received[0] = after(received[0], own_up)
    packed_seed = call(pack_kernel, "pack", (scalars, seed, *received), packed)
    seed_up = from_up(packed_seed)
    seed_cross = [from_group(packed_seed, step) for step in steps]
    cross0 = call(
        functools.partial(cross_kernel, weight), "cross", (embeddings, *cross_own), like((len(steps) * rows, rows), BF16)
    )
    across_a = from_core(side_a)
    unit_stack = like((QUAD * rows, depth), BF16)
    units, seed_stack = call(
        stage_seed_kernel,
        "stage_own",
        (clusters, embeddings, side_a, own_core, across_a, packed_seed),
        (unit_stack, like((QUAD * rows, classes // QUAD), BF16)),
    )
    side_b = after(side_b, (cross0, units, up_side_a))
    across_b = from_core(side_b)
    up_core, up_across_a = from_core(own_up), from_core(up_side_a)
    up_units = call(
        stage_kernel, "stage_up", (clusters, after(own_up, side_b), up_side_a, up_core, up_across_a), unit_stack
    )
    cross0 = after(cross0, (side_b, seed_up, seed_cross))
    cross1, cross2 = from_side(cross0), from_core(cross0)
    units, _, far, sums = call(
        far_kernel,
        "far",
        (clusters, units, up_units, side_b, across_b, seed_stack),
        (unit_stack, unit_stack, matrix, packed),
        aliases={1: 0, 2: 1},
    )
    near = call(near_kernel, "near", (units,), matrix)
    cross3 = from_core(after(cross1, near))

    sent = from_down(sums)
    crosses = (cross0, cross1, cross2, cross3)
    kept = call(
        gather_kernel,
        "gather",
        (clusters, near, far, *crosses, packed_seed, seed_up, *seed_cross),
        like(labels.shape, F32),
        [stack, total],
    )
    tail_rows = rows // 96 * 16
    head = like((rows - tail_rows, classes), BF16)
    tail = like((tail_rows + 2 * FACTORS, classes), BF16)
    summed, head, squares = call(
        combine_kernel, "combine", (scalars, kept, sent), (packed, head, like((FACTORS, rows), F32))
    )

    head_up = from_up(head)
    head_cross = [from_group(head, step) for step in steps]
    half, half_piece = like((half_rows, classes), BF16), like((half_rows, classes // QUAD), BF16)
    tail, _, current_stack, sums_b, sums_a, *pieces = call(
        mix_kernel,
        "mix",
        (scalars, far, summed, squares, *exchange([squares] * 3), packed_seed),
        (
            tail, packed, like((QUAD * rows, classes // QUAD), BF16),
            half, half, half_piece, half_piece, half_piece,
        ),
    )
    received = exchange(pieces)
    near_total = call(
        near_products,
        "near_products",
        (near, after(current_stack, received[0])),
        like((QUAD * rows, classes // QUAD), F32),
    )
    tail_up = from_up(tail)
    tail_cross = [from_group(after(tail, near_total), step) for step in steps]
    sent_b = from_down(sums_b)
    sums_a = call(pack_kernel, "pack", (scalars, sums_a, *received), half)
    sums_a = after(sums_a, (head_up, head_cross, tail_up, tail_cross))
    sent_a = from_down(sums_a)
    head_up = after(head_up, sums_a)
    triples = [head_up, tail_up, seed_up]
    for top, rest, own in zip(head_cross, tail_cross, seed_cross):
        triples += [top, rest, own]
    _, kept_b, kept_a, *pieces = call(
        gather_mixed_kernel,
        "gather_mixed",
        (clusters, far, *crosses, near_total, *triples),
        (
            like((QUAD * rows, classes // QUAD), F32),
            like(half.shape, F32), half, half_piece, half_piece, half_piece,
        ),
        [pltpu.VMEM(labels.shape, BF16), stack],
        aliases={6: 0},
    )
    received = exchange(pieces)
    sums_b, *pieces = call(add_kernel, "add", (scalars, after(kept_b, received[0]), sent_b), (half, half_piece, half_piece, half_piece))
    kept_a = call(pack_kernel, "pack", (scalars, kept_a, *received), half)
    return call(
        finish_kernel,
        "finish",
        (scalars, kept_a, sent_a, sums_b, *exchange(pieces), seed),
        packed,
        [pltpu.VMEM(half.shape, BF16)],
    )


def solution(mesh):
    placed = (P(("grp", "dev"), None), P(("grp", "dev"), None), P(("grp", "dev")))
    return jax.shard_map(
        body, mesh=mesh, in_specs=placed, out_specs=P(("grp", "dev"), None), check_vma=False
    )
```

```python
import functools
import math

import jax
import jax.numpy as jnp
from jax import lax
from jax.experimental import pallas as pl
from jax.experimental.pallas import tpu as pltpu
from jax.sharding import PartitionSpec as P

sharpness = 25.0
keep_share = 0.8
BF16 = jnp.bfloat16
F32 = jnp.float32
QUAD = 4
INVALID = 1e38
FACTORS = 8
MB = 2**20


def along_dev(block, source):
    size = lax.axis_size("dev")
    return lax.ppermute(block, "dev", [(source(i) % size, i) for i in range(size)])


def from_up(block):
    return along_dev(block, lambda i: i + QUAD)


def from_down(block):
    return along_dev(block, lambda i: i - QUAD)


def from_side(block):
    return along_dev(block, lambda i: i ^ 2)


def from_core(block):
    return along_dev(block, lambda i: i ^ 1)


def from_group(block, step):
    size = lax.axis_size("grp")
    return lax.ppermute(block, "grp", [((i + step) % size, i) for i in range(size)])


def after(value, earlier):
    return lax.optimization_barrier((value, earlier))[0]


def exchange(pieces):
    return [along_dev(piece, lambda i, m=m: i ^ m) for m, piece in enumerate(pieces, 1)]


def call(kernel, name, operands, out_shape, scratch=(), limit=12, aliases={}):
    specs = [
        pl.BlockSpec(memory_space=pltpu.SMEM if x.dtype == jnp.int32 else pltpu.VMEM) for x in operands
    ]
    return pl.pallas_call(
        kernel,
        in_specs=specs,
        out_shape=out_shape,
        scratch_shapes=list(scratch),
        input_output_aliases=aliases,
        compiler_params=pltpu.CompilerParams(vmem_limit_bytes=limit * MB),
        name=name,
    )(*operands)


def like(shape, dtype):
    return jax.ShapeDtypeStruct(tuple(shape), dtype)


def dot(left, right):
    return jnp.dot(left, right, preferred_element_type=F32)


def affinity(left, right):
    cosine = lax.dot_general(left, right, (((1,), (1,)), ((), ())), preferred_element_type=F32)
    return jnp.exp2(cosine * (sharpness * math.log2(math.e)))


def cut(block, place, pieces):
    quarter = block.shape[1] // QUAD
    for k in range(QUAD):
        for m, piece in pieces:

            @pl.when(place ^ m == k)
            def _():
                piece[...] = block[:, k * quarter : (k + 1) * quarter]


def join(place, pieces, out):
    quarter = out.shape[1] // QUAD
    for k in range(QUAD):
        for m, piece in pieces:

            @pl.when(place ^ m == k)
            def _():
                out[:, k * quarter : (k + 1) * quarter] = piece[...]


def unit_rows(embeddings):
    values = embeddings.astype(F32)
    scaled = values * lax.rsqrt(jnp.mean(values * values, axis=-1, keepdims=True) + 1e-06)
    return (scaled / math.sqrt(values.shape[-1])).astype(BF16)


def seed_kernel(scalars, labels, seed, *pieces):
    row = lax.broadcasted_iota(jnp.int32, labels.shape, 0)
    seed[...] = jnp.where(row < scalars[1], labels[...].astype(F32), 0.0).astype(BF16)
    cut(seed, scalars[0], list(enumerate(pieces, 1)))


def pack_kernel(scalars, whole, p1, p2, p3, out):
    out[...] = whole[...]
    join(scalars[0], [(1, p1), (2, p2), (3, p3)], out)


def at(cluster, rows):
    return pl.ds(pl.multiple_of(cluster * rows, rows), rows)


def place_units(start, block, stack):
    count = block.shape[0]
    stack[pl.ds(pl.multiple_of(start, count), count), :] = unit_rows(block[...])


def near_kernel(units, near):
    rows = units.shape[0] // QUAD
    for k in range(QUAD):
        for pair in range(2):
            span = slice(2 * pair * rows, 2 * (pair + 1) * rows)
            tile = affinity(units[k * rows : (k + 1) * rows, :], units[span, :])
            if k // 2 == pair:
                row = lax.broadcasted_iota(jnp.int32, tile.shape, 0)
                lane = lax.broadcasted_iota(jnp.int32, tile.shape, 1)
                tile = jnp.where(row + (k % 2) * rows == lane, 0.0, tile)
            near[k * rows : (k + 1) * rows, span] = tile.astype(BF16)


def stage_kernel(clusters, own, side, core, across, units):
    rows = own.shape[0]
    for i, block in enumerate((own, side, core, across)):
        place_units(clusters[i] * rows, block, units)


def stage_seed_kernel(clusters, own, side, core, across, seed, units, stack):
    stage_kernel(clusters, own, side, core, across, units)
    unpack(seed, stack)


def far_kernel(clusters, units, up_in, side_b, across_b, stack, up_units, far, sums):
    rows = units.shape[0] // QUAD
    for i, block in ((1, side_b), (3, across_b)):
        place_units((clusters[i] + 1) * rows - block.shape[0], block, up_units)
    for k in range(QUAD):
        here = slice(k * rows, (k + 1) * rows)
        for first in range(0, k + 1, 2):
            span = slice(first * rows, min(first + 2, k + 1) * rows)
            far[here, span] = affinity(units[here, :], up_units[span, :]).astype(BF16)
    scatter(far, stack, (sums,))


def unpack(block, stack):
    rows, quarter = stack.shape[0] // QUAD, stack.shape[1]
    for k in range(QUAD):
        stack[k * rows : (k + 1) * rows, :] = block[:, k * quarter : (k + 1) * quarter]


def scatter(far, stack, outs):
    rows, quarter = stack.shape[0] // QUAD, stack.shape[1]
    for k in range(QUAD):
        total = lax.dot_general(
            far[k * rows :, k * rows : (k + 1) * rows],
            stack[k * rows :, :],
            (((0,), (0,)), ((), ())),
            preferred_element_type=F32,
        )
        first = 0
        for out in outs:
            out[:, k * quarter : (k + 1) * quarter] = total[first : first + out.shape[0], :].astype(out.dtype)
            first = first + out.shape[0]


def mix_kernel(scalars, far, summed, s0, s1, s2, s3, seed, tail, mixed, stack, out_b, out_a, p1, p2, p3):
    total = (s0[...] + s1[...]) + (s2[...] + s3[...])
    rows = summed.shape[0]
    kept = tail.shape[0] - 2 * FACTORS
    factor = jnp.where(total > INVALID / 10, 0.0, lax.rsqrt(total / summed.shape[1] + 1e-06))
    high = factor.astype(BF16).astype(F32)
    tail[:kept, :] = summed[rows - kept :, :]
    tail[kept:, :] = jnp.zeros((2 * FACTORS, tail.shape[1]), BF16)
    tail[kept:, :rows] = jnp.concatenate([high, factor - high]).astype(BF16)
    mix(summed.at[: rows - kept], tail, seed, mixed)
    unpack(mixed, stack)
    scatter(far, stack, (out_a, out_b))
    cut(out_a, scalars[0], [(1, p1), (2, p2), (3, p3)])


def cross_kernel(weight, own, *rest):
    others, out = rest[:-1], rest[-1]
    rows = own.shape[0]
    unit = unit_rows(own[...])
    for n, other in enumerate(others):
        out[n * rows : (n + 1) * rows, :] = (affinity(unit, unit_rows(other[...])) * weight).astype(BF16)


def near_products(near, stack, total):
    rows = stack.shape[0] // QUAD
    for k in range(QUAD):
        here = slice(k * rows, (k + 1) * rows)
        total[here, :] = dot(near[here, :], stack[...])


def cross_products(clusters, tiles, n, stack, total):
    rows = stack.shape[0] // QUAD
    for i, tile in enumerate(tiles):
        here = at(clusters[i], rows)
        total[here, :] += dot(tile[n * rows : (n + 1) * rows, :], stack[here, :])


def far_products(far, stack, total, outs):
    rows, quarter = stack.shape[0] // QUAD, stack.shape[1]
    for k in range(QUAD):
        here = slice(k * rows, (k + 1) * rows)
        done = total[here, :] + dot(far[here, : (k + 1) * rows], stack[: (k + 1) * rows, :])
        first = 0
        for out in outs:
            out[:, k * quarter : (k + 1) * quarter] = done[first : first + out.shape[0], :].astype(out.dtype)
            first = first + out.shape[0]


def gather_kernel(clusters, near, far, t0, t1, t2, t3, own, up, *rest):
    cross, (out, stack, total) = rest[:-3], rest[-3:]
    unpack(own, stack)
    near_products(near, stack, total)
    for n, block in enumerate(cross):
        unpack(block, stack)
        cross_products(clusters, (t0, t1, t2, t3), n, stack, total)
    unpack(up, stack)
    far_products(far, stack, total, (out,))


def gather_mixed_kernel(clusters, far, t0, t1, t2, t3, total_in, *rest):
    triples, (total, out_b, out_a, p1, p2, p3, mixed, stack) = rest[:-8], rest[-8:]
    triples = [triples[i : i + 3] for i in range(0, len(triples), 3)]
    for n, triple in enumerate(triples[1:]):
        mix(*triple, mixed)
        unpack(mixed, stack)
        cross_products(clusters, (t0, t1, t2, t3), n, stack, total)
    mix(*triples[0], mixed)
    unpack(mixed, stack)
    far_products(far, stack, total, (out_a, out_b))
    cut(out_a, clusters[0], [(1, p1), (2, p2), (3, p3)])


def lanes_of(count, lanes):
    quarter = lanes // QUAD
    row = lax.broadcasted_iota(jnp.int32, (count, lanes), 0) & (FACTORS - 1)
    lane = lax.broadcasted_iota(jnp.int32, (count, lanes), 1)
    return ((lane >= row * quarter) & (lane < (row + 1) * quarter)).astype(F32).astype(BF16)


def mix(head, tail, seed, out):
    rows, lanes = seed.shape
    first = head.shape[0]
    kept = rows - first
    spread = lax.dot_general(
        tail[kept:, :rows],
        lanes_of(2 * FACTORS, lanes),
        (((0,), (0,)), ((), ())),
        preferred_element_type=F32,
    )
    for block, start, stop in ((head[...], 0, first), (tail[:kept, :], first, rows)):
        share = keep_share * block.astype(F32) * spread[start:stop, :]
        out[start:stop, :] = (share + (1.0 - keep_share) * seed[start:stop, :].astype(F32)).astype(BF16)


def combine_kernel(scalars, kept, sent, summed, head, squares):
    total = kept[...] + sent[...].astype(F32)
    summed[...] = total.astype(BF16)
    head[...] = summed[: head.shape[0], :]
    square = total * total
    high = square.astype(BF16)
    marks = lanes_of(2 * FACTORS, total.shape[1])
    sums = sum(
        lax.dot_general(marks, part, (((1,), (1,)), ((), ())), preferred_element_type=F32)
        for part in (high, (square - high.astype(F32)).astype(BF16))
    )
    row = lax.broadcasted_iota(jnp.int32, sums.shape, 0)
    lane = lax.broadcasted_iota(jnp.int32, sums.shape, 1)
    sums = sums + jnp.where((row == scalars[0]) & (lane >= scalars[1]), INVALID, 0.0)
    squares[...] = sums[:FACTORS, :]


def add_kernel(scalars, kept, sent, out, p1, p2, p3):
    out[...] = (kept[...] + sent[...].astype(F32)).astype(BF16)
    cut(out, scalars[0], [(1, p1), (2, p2), (3, p3)])


def finished(scalars, summed, seed, first):
    factor = lax.rsqrt(jnp.mean(summed * summed, axis=-1, keepdims=True) + 1e-06)
    result = keep_share * summed * factor + (1.0 - keep_share) * seed[...].astype(F32)
    row = lax.broadcasted_iota(jnp.int32, summed.shape, 0) + first
    return jnp.where(row < scalars[1], result, 0.0).astype(BF16)


def finish_b_kernel(scalars, sums, p1, p2, p3, seed, out, whole):
    whole[...] = sums[...]
    join(scalars[0], [(1, p1), (2, p2), (3, p3)], whole)
    out[...] = finished(scalars, whole[...].astype(F32), seed, sums.shape[0])


def finish_a_kernel(scalars, out_b, kept, sent, seed, out):
    out[...] = finished(scalars, kept[...].astype(F32) + sent[...].astype(F32), seed, 0)


def finish(kernel, name, half, operands, whole, scratch=(), aliases={}):
    rows, classes = whole.shape
    block = (rows // 2, classes)

    def spec(i, x):
        if x.dtype == jnp.int32:
            return pl.BlockSpec(memory_space=pltpu.SMEM)
        if i in aliases:
            return pl.BlockSpec(memory_space=pl.ANY)
        return pl.BlockSpec(block, lambda _: (half, 0)) if x.shape == whole.shape else pl.BlockSpec(x.shape, lambda _: (0, 0))

    return pl.pallas_call(
        kernel,
        grid=(1,),
        in_specs=[spec(i, x) for i, x in enumerate(operands)],
        out_specs=pl.BlockSpec(block, lambda _: (half, 0)),
        out_shape=whole,
        scratch_shapes=list(scratch),
        input_output_aliases=aliases,
        compiler_params=pltpu.CompilerParams(vmem_limit_bytes=12 * MB),
        name=name,
    )(*operands)


def body(embeddings, labels, cluster_rows):
    rows, classes = labels.shape
    depth = embeddings.shape[1]
    groups = lax.axis_size("grp")
    steps, weight = ([1], 2.0) if groups == 2 else ([1, -1], 1.0)
    place = (lax.axis_index("dev") % QUAD).astype(jnp.int32)
    clusters = jnp.stack([place, place ^ 2, place ^ 1, place ^ 3])
    scalars = jnp.stack([place, cluster_rows[0]])
    stack = pltpu.VMEM((QUAD * rows, classes // QUAD), BF16)
    total = pltpu.VMEM((QUAD * rows, classes // QUAD), F32)
    packed = like(labels.shape, BF16)
    piece = like((rows, classes // QUAD), BF16)
    matrix = like((QUAD * rows, QUAD * rows), BF16)

    half_rows = rows // 2

    side = from_side(embeddings)
    own_up = from_up(embeddings)
    seed, *pieces = call(seed_kernel, "seed", (scalars, labels), (packed, piece, piece, piece))
    received = exchange(pieces)
    own_core = from_core(embeddings)
    cross_own = [from_group(after(embeddings, seed), step) for step in steps]
    up_side_a = from_up(side[:half_rows])
    side_b = from_side(after(own_up[half_rows:], received[1:]))
    received[0] = after(received[0], own_up)
    packed_seed = call(pack_kernel, "pack", (scalars, seed, *received), packed)
    seed_up = from_up(packed_seed)
    seed_cross = [from_group(after(packed_seed, up_side_a), step) for step in steps]
    cross0 = call(
        functools.partial(cross_kernel, weight), "cross", (embeddings, *cross_own), like((len(steps) * rows, rows), BF16)
    )
    across = from_core(side)
    unit_stack = like((QUAD * rows, depth), BF16)
    units, seed_stack = call(
        stage_seed_kernel,
        "stage_own",
        (clusters, embeddings, side, own_core, across, packed_seed),
        (unit_stack, like((QUAD * rows, classes // QUAD), BF16)),
    )
    side_b = after(side_b, (cross0, units, up_side_a))
    across_b = from_core(side_b)
    up_core, up_across_a = from_core(own_up), from_core(up_side_a)
    up_units = call(
        stage_kernel, "stage_up", (clusters, after(own_up, side_b), up_side_a, up_core, up_across_a), unit_stack
    )
    cross0 = after(cross0, (side_b, seed_up, seed_cross))
    cross1, cross2 = from_side(cross0), from_core(cross0)
    _, far, sums = call(
        far_kernel,
        "far",
        (clusters, units, up_units, side_b, across_b, seed_stack),
        (unit_stack, matrix, packed),
        aliases={2: 0},
    )
    near = call(near_kernel, "near", (after(units, sums),), matrix)
    cross3 = from_core(after(cross1, near))

    sent = from_down(sums)
    crosses = (cross0, cross1, cross2, cross3)
    kept = call(
        gather_kernel,
        "gather",
        (clusters, near, far, *crosses, packed_seed, seed_up, *seed_cross),
        like(labels.shape, F32),
        [stack, total],
    )
    tail_rows = rows // 96 * 16
    head = like((rows - tail_rows, classes), BF16)
    tail = like((tail_rows + 2 * FACTORS, classes), BF16)
    summed, head, squares = call(
        combine_kernel, "combine", (scalars, kept, sent), (packed, head, like((FACTORS, rows), F32))
    )

    head_up = from_up(head)
    head_cross = [from_group(head, step) for step in steps]
    half, half_piece = like((half_rows, classes), BF16), like((half_rows, classes // QUAD), BF16)
    tail, _, current_stack, sums_b, sums_a, *pieces = call(
        mix_kernel,
        "mix",
        (scalars, far, summed, squares, *exchange([squares] * 3), packed_seed),
        (
            tail, packed, like((QUAD * rows, classes // QUAD), BF16),
            half, half, half_piece, half_piece, half_piece,
        ),
    )
    received = exchange(pieces)
    near_total = call(
        near_products,
        "near_products",
        (near, after(current_stack, received[0])),
        like((QUAD * rows, classes // QUAD), F32),
    )
    tail_up = from_up(tail)
    tail_cross = [from_group(after(tail, near_total), step) for step in steps]
    sent_b = from_down(sums_b)
    sums_a = call(pack_kernel, "pack", (scalars, sums_a, *received), half)
    sums_a = after(sums_a, (head_up, head_cross, tail_up, tail_cross))
    sent_a = from_down(sums_a)
    head_up = after(head_up, sums_a)
    triples = [head_up, tail_up, seed_up]
    for top, rest, own in zip(head_cross, tail_cross, seed_cross):
        triples += [top, rest, own]
    _, kept_b, kept_a, *pieces = call(
        gather_mixed_kernel,
        "gather_mixed",
        (clusters, far, *crosses, near_total, *triples),
        (
            like((QUAD * rows, classes // QUAD), F32),
            like(half.shape, F32), half, half_piece, half_piece, half_piece,
        ),
        [pltpu.VMEM(labels.shape, BF16), stack],
        aliases={6: 0},
    )
    received = exchange(pieces)
    sums_b, *pieces = call(add_kernel, "add", (scalars, after(kept_b, received[0]), sent_b), (half, half_piece, half_piece, half_piece))
    kept_a = call(pack_kernel, "pack", (scalars, kept_a, *received), half)
    result = finish(
        finish_b_kernel,
        "finish_b",
        1,
        (scalars, sums_b, *exchange(pieces), seed),
        packed,
        [pltpu.VMEM(half.shape, BF16)],
    )
    return finish(finish_a_kernel, "finish_a", 0, (scalars, result, kept_a, sent_a, seed), packed, aliases={1: 0})


def solution(mesh):
    placed = (P(("grp", "dev"), None), P(("grp", "dev"), None), P(("grp", "dev")))
    return jax.shard_map(
        body, mesh=mesh, in_specs=placed, out_specs=P(("grp", "dev"), None), check_vma=False
    )
```

```python
import functools
import math

import jax
import jax.numpy as jnp
from jax import lax
from jax.experimental import pallas as pl
from jax.experimental.pallas import tpu as pltpu
from jax.sharding import PartitionSpec as P

sharpness = 25.0
keep_share = 0.8
BF16 = jnp.bfloat16
F32 = jnp.float32
QUAD = 4
INVALID = 1e38
FACTORS = 8
MB = 2**20


def along_dev(block, source):
    size = lax.axis_size("dev")
    return lax.ppermute(block, "dev", [(source(i) % size, i) for i in range(size)])


def from_up(block):
    return along_dev(block, lambda i: i + QUAD)


def from_down(block):
    return along_dev(block, lambda i: i - QUAD)


def from_side(block):
    return along_dev(block, lambda i: i ^ 2)


def from_core(block):
    return along_dev(block, lambda i: i ^ 1)


def from_group(block, step):
    size = lax.axis_size("grp")
    return lax.ppermute(block, "grp", [((i + step) % size, i) for i in range(size)])


def after(value, earlier):
    return lax.optimization_barrier((value, earlier))[0]


def exchange(pieces):
    return [along_dev(piece, lambda i, m=m: i ^ m) for m, piece in enumerate(pieces, 1)]


def call(kernel, name, operands, out_shape, scratch=(), limit=12, aliases={}):
    specs = [
        pl.BlockSpec(memory_space=pltpu.SMEM if x.dtype == jnp.int32 else pltpu.VMEM) for x in operands
    ]
    return pl.pallas_call(
        kernel,
        in_specs=specs,
        out_shape=out_shape,
        scratch_shapes=list(scratch),
        input_output_aliases=aliases,
        compiler_params=pltpu.CompilerParams(vmem_limit_bytes=limit * MB),
        name=name,
    )(*operands)


def like(shape, dtype):
    return jax.ShapeDtypeStruct(tuple(shape), dtype)


def dot(left, right):
    return jnp.dot(left, right, preferred_element_type=F32)


def affinity(left, right):
    cosine = lax.dot_general(left, right, (((1,), (1,)), ((), ())), preferred_element_type=F32)
    return jnp.exp2(cosine * (sharpness * math.log2(math.e)))


def cut(block, place, pieces):
    quarter = block.shape[1] // QUAD
    for k in range(QUAD):
        for m, piece in pieces:

            @pl.when(place ^ m == k)
            def _():
                piece[...] = block[:, k * quarter : (k + 1) * quarter]


def join(place, pieces, out):
    quarter = out.shape[1] // QUAD
    for k in range(QUAD):
        for m, piece in pieces:

            @pl.when(place ^ m == k)
            def _():
                out[:, k * quarter : (k + 1) * quarter] = piece[...]


def unit_rows(embeddings):
    values = embeddings.astype(F32)
    scaled = values * lax.rsqrt(jnp.mean(values * values, axis=-1, keepdims=True) + 1e-06)
    return (scaled / math.sqrt(values.shape[-1])).astype(BF16)


def seed_kernel(scalars, labels, seed, *pieces):
    row = lax.broadcasted_iota(jnp.int32, labels.shape, 0)
    seed[...] = jnp.where(row < scalars[1], labels[...].astype(F32), 0.0).astype(BF16)
    cut(seed, scalars[0], list(enumerate(pieces, 1)))


def pack_kernel(scalars, whole, p1, p2, p3, out):
    out[...] = whole[...]
    join(scalars[0], [(1, p1), (2, p2), (3, p3)], out)


def at(cluster, rows):
    return pl.ds(pl.multiple_of(cluster * rows, rows), rows)


def place_units(start, block, stack):
    count = block.shape[0]
    stack[pl.ds(pl.multiple_of(start, count), count), :] = unit_rows(block[...])


def near_kernel(units, near):
    rows = units.shape[0] // QUAD
    for k in range(QUAD):
        for pair in range(2):
            span = slice(2 * pair * rows, 2 * (pair + 1) * rows)
            tile = affinity(units[k * rows : (k + 1) * rows, :], units[span, :])
            if k // 2 == pair:
                row = lax.broadcasted_iota(jnp.int32, tile.shape, 0)
                lane = lax.broadcasted_iota(jnp.int32, tile.shape, 1)
                tile = jnp.where(row + (k % 2) * rows == lane, 0.0, tile)
            near[k * rows : (k + 1) * rows, span] = tile.astype(BF16)


def stage_kernel(clusters, own, side_a, core, across_a, units):
    rows = own.shape[0]
    for i, block in enumerate((own, side_a, core, across_a)):
        place_units(clusters[i] * rows, block, units)


def stage_seed_kernel(clusters, own, side_a, core, across_a, seed, units, stack):
    stage_kernel(clusters, own, side_a, core, across_a, units)
    unpack(seed, stack)


def far_kernel(clusters, units_in, up_in, side_b, across_b, stack, units, up_units, far, sums):
    rows = units.shape[0] // QUAD
    half = rows // 2
    for i, block in ((1, side_b), (3, across_b)):
        start = clusters[i] * rows + half
        place_units(start, block.at[:half], units)
        place_units(start, block.at[half:], up_units)
    for k in range(QUAD):
        here = slice(k * rows, (k + 1) * rows)
        for first in range(0, k + 1, 2):
            span = slice(first * rows, min(first + 2, k + 1) * rows)
            far[here, span] = affinity(units[here, :], up_units[span, :]).astype(BF16)
    scatter(far, stack, (sums,))


def unpack(block, stack):
    rows, quarter = stack.shape[0] // QUAD, stack.shape[1]
    for k in range(QUAD):
        stack[k * rows : (k + 1) * rows, :] = block[:, k * quarter : (k + 1) * quarter]


def scatter(far, stack, outs):
    rows, quarter = stack.shape[0] // QUAD, stack.shape[1]
    for k in range(QUAD):
        total = lax.dot_general(
            far[k * rows :, k * rows : (k + 1) * rows],
            stack[k * rows :, :],
            (((0,), (0,)), ((), ())),
            preferred_element_type=F32,
        )
        first = 0
        for out in outs:
            out[:, k * quarter : (k + 1) * quarter] = total[first : first + out.shape[0], :].astype(out.dtype)
            first = first + out.shape[0]


def mix_kernel(scalars, far, summed, s0, s1, s2, s3, seed, tail, mixed, stack, out_b, out_a, p1, p2, p3):
    total = (s0[...] + s1[...]) + (s2[...] + s3[...])
    rows = summed.shape[0]
    kept = tail.shape[0] - 2 * FACTORS
    factor = jnp.where(total > INVALID / 10, 0.0, lax.rsqrt(total / summed.shape[1] + 1e-06))
    high = factor.astype(BF16).astype(F32)
    tail[:kept, :] = summed[rows - kept :, :]
    tail[kept:, :] = jnp.zeros((2 * FACTORS, tail.shape[1]), BF16)
    tail[kept:, :rows] = jnp.concatenate([high, factor - high]).astype(BF16)
    mix(summed.at[: rows - kept], tail, seed, mixed)
    unpack(mixed, stack)
    scatter(far, stack, (out_a, out_b))
    cut(out_a, scalars[0], [(1, p1), (2, p2), (3, p3)])


def cross_kernel(weight, own, *rest):
    others, out = rest[:-1], rest[-1]
    rows = own.shape[0]
    unit = unit_rows(own[...])
    for n, other in enumerate(others):
        out[n * rows : (n + 1) * rows, :] = (affinity(unit, unit_rows(other[...])) * weight).astype(BF16)


def near_products(near, stack, total):
    rows = stack.shape[0] // QUAD
    for k in range(QUAD):
        here = slice(k * rows, (k + 1) * rows)
        total[here, :] = dot(near[here, :], stack[...])


def cross_products(clusters, tiles, n, stack, total):
    rows = stack.shape[0] // QUAD
    for i, tile in enumerate(tiles):
        here = at(clusters[i], rows)
        total[here, :] += dot(tile[n * rows : (n + 1) * rows, :], stack[here, :])


def far_products(far, stack, total, outs):
    rows, quarter = stack.shape[0] // QUAD, stack.shape[1]
    for k in range(QUAD):
        here = slice(k * rows, (k + 1) * rows)
        done = total[here, :] + dot(far[here, : (k + 1) * rows], stack[: (k + 1) * rows, :])
        first = 0
        for out in outs:
            out[:, k * quarter : (k + 1) * quarter] = done[first : first + out.shape[0], :].astype(out.dtype)
            first = first + out.shape[0]


def gather_kernel(clusters, near, far, t0, t1, t2, t3, own, up, *rest):
    cross, (out, stack, total) = rest[:-3], rest[-3:]
    unpack(own, stack)
    near_products(near, stack, total)
    for n, block in enumerate(cross):
        unpack(block, stack)
        cross_products(clusters, (t0, t1, t2, t3), n, stack, total)
    unpack(up, stack)
    far_products(far, stack, total, (out,))


def gather_mixed_kernel(clusters, far, t0, t1, t2, t3, total_in, *rest):
    triples, (total, out_b, out_a, p1, p2, p3, mixed, stack) = rest[:-8], rest[-8:]
    triples = [triples[i : i + 3] for i in range(0, len(triples), 3)]
    for n, triple in enumerate(triples[1:]):
        mix(*triple, mixed)
        unpack(mixed, stack)
        cross_products(clusters, (t0, t1, t2, t3), n, stack, total)
    mix(*triples[0], mixed)
    unpack(mixed, stack)
    far_products(far, stack, total, (out_a, out_b))
    cut(out_a, clusters[0], [(1, p1), (2, p2), (3, p3)])


def lanes_of(count, lanes):
    quarter = lanes // QUAD
    row = lax.broadcasted_iota(jnp.int32, (count, lanes), 0) & (FACTORS - 1)
    lane = lax.broadcasted_iota(jnp.int32, (count, lanes), 1)
    return ((lane >= row * quarter) & (lane < (row + 1) * quarter)).astype(F32).astype(BF16)


def mix(head, tail, seed, out):
    rows, lanes = seed.shape
    first = head.shape[0]
    kept = rows - first
    spread = lax.dot_general(
        tail[kept:, :rows],
        lanes_of(2 * FACTORS, lanes),
        (((0,), (0,)), ((), ())),
        preferred_element_type=F32,
    )
    for block, start, stop in ((head[...], 0, first), (tail[:kept, :], first, rows)):
        share = keep_share * block.astype(F32) * spread[start:stop, :]
        out[start:stop, :] = (share + (1.0 - keep_share) * seed[start:stop, :].astype(F32)).astype(BF16)


def combine_kernel(scalars, kept, sent, summed, head, squares):
    total = kept[...] + sent[...].astype(F32)
    summed[...] = total.astype(BF16)
    head[...] = summed[: head.shape[0], :]
    square = total * total
    high = square.astype(BF16)
    marks = lanes_of(2 * FACTORS, total.shape[1])
    sums = sum(
        lax.dot_general(marks, part, (((1,), (1,)), ((), ())), preferred_element_type=F32)
        for part in (high, (square - high.astype(F32)).astype(BF16))
    )
    row = lax.broadcasted_iota(jnp.int32, sums.shape, 0)
    lane = lax.broadcasted_iota(jnp.int32, sums.shape, 1)
    sums = sums + jnp.where((row == scalars[0]) & (lane >= scalars[1]), INVALID, 0.0)
    squares[...] = sums[:FACTORS, :]


def add_kernel(scalars, kept, sent, out, p1, p2, p3):
    out[...] = (kept[...] + sent[...].astype(F32)).astype(BF16)
    cut(out, scalars[0], [(1, p1), (2, p2), (3, p3)])


def finished(scalars, summed, seed, first):
    factor = lax.rsqrt(jnp.mean(summed * summed, axis=-1, keepdims=True) + 1e-06)
    result = keep_share * summed * factor + (1.0 - keep_share) * seed[...].astype(F32)
    row = lax.broadcasted_iota(jnp.int32, summed.shape, 0) + first
    return jnp.where(row < scalars[1], result, 0.0).astype(BF16)


def finish_b_kernel(scalars, sums, p1, p2, p3, seed, out, whole):
    whole[...] = sums[...]
    join(scalars[0], [(1, p1), (2, p2), (3, p3)], whole)
    out[...] = finished(scalars, whole[...].astype(F32), seed, sums.shape[0])


def finish_a_kernel(scalars, out_b, kept, sent, seed, out):
    out[...] = finished(scalars, kept[...].astype(F32) + sent[...].astype(F32), seed, 0)


def finish(kernel, name, half, operands, whole, scratch=(), aliases={}):
    rows, classes = whole.shape
    block = (rows // 2, classes)

    def spec(i, x):
        if x.dtype == jnp.int32:
            return pl.BlockSpec(memory_space=pltpu.SMEM)
        if i in aliases:
            return pl.BlockSpec(memory_space=pl.ANY)
        return pl.BlockSpec(block, lambda _: (half, 0)) if x.shape == whole.shape else pl.BlockSpec(x.shape, lambda _: (0, 0))

    return pl.pallas_call(
        kernel,
        grid=(1,),
        in_specs=[spec(i, x) for i, x in enumerate(operands)],
        out_specs=pl.BlockSpec(block, lambda _: (half, 0)),
        out_shape=whole,
        scratch_shapes=list(scratch),
        input_output_aliases=aliases,
        compiler_params=pltpu.CompilerParams(vmem_limit_bytes=12 * MB),
        name=name,
    )(*operands)


def body(embeddings, labels, cluster_rows):
    rows, classes = labels.shape
    depth = embeddings.shape[1]
    groups = lax.axis_size("grp")
    steps, weight = ([1], 2.0) if groups == 2 else ([1, -1], 1.0)
    place = (lax.axis_index("dev") % QUAD).astype(jnp.int32)
    clusters = jnp.stack([place, place ^ 2, place ^ 1, place ^ 3])
    scalars = jnp.stack([place, cluster_rows[0]])
    stack = pltpu.VMEM((QUAD * rows, classes // QUAD), BF16)
    total = pltpu.VMEM((QUAD * rows, classes // QUAD), F32)
    packed = like(labels.shape, BF16)
    piece = like((rows, classes // QUAD), BF16)
    matrix = like((QUAD * rows, QUAD * rows), BF16)

    half_rows = rows // 2

    own_up = from_up(embeddings)
    side_a = from_side(embeddings[:half_rows])
    seed, *pieces = call(seed_kernel, "seed", (scalars, labels), (packed, piece, piece, piece))
    received = exchange(pieces)
    own_core = from_core(embeddings)
    cross_own = [from_group(after(embeddings, seed), step) for step in steps]
    up_side_a = from_up(side_a)
    late = jnp.concatenate([after(embeddings, side_a)[half_rows:], own_up[half_rows:]])
    side_b = from_side(after(late, received))
    received[0] = after(received[0], own_up)
    packed_seed = call(pack_kernel, "pack", (scalars, seed, *received), packed)
    seed_up = from_up(packed_seed)
    across_a = from_core(side_a)
    unit_stack = like((QUAD * rows, depth), BF16)
    units, seed_stack = call(
        stage_seed_kernel,
        "stage_own",
        (clusters, embeddings, side_a, own_core, across_a, packed_seed),
        (unit_stack, like((QUAD * rows, classes // QUAD), BF16)),
    )
    seed_cross = [from_group(after(packed_seed, (cross_own, units)), step) for step in steps]
    side_b = after(side_b, (units, up_side_a))
    across_b = from_core(side_b)
    up_core, up_across_a = from_core(own_up), from_core(up_side_a)
    up_units = call(
        stage_kernel, "stage_up", (clusters, after(own_up, side_b), up_side_a, up_core, up_across_a), unit_stack
    )
    units, _, far, sums = call(
        far_kernel,
        "far",
        (clusters, units, up_units, side_b, across_b, seed_stack),
        (unit_stack, unit_stack, matrix, packed),
        aliases={1: 0, 2: 1},
    )
    cross0 = call(
        functools.partial(cross_kernel, weight), "cross", (after(embeddings, (sums, seed_up)), *cross_own), like((len(steps) * rows, rows), BF16)
    )
    cross0 = after(cross0, seed_cross)
    cross1, cross2 = from_side(cross0), from_core(cross0)
    near = call(near_kernel, "near", (units,), matrix)
    cross3 = from_core(after(cross1, near))

    sent = from_down(sums)
    crosses = (cross0, cross1, cross2, cross3)
    kept = call(
        gather_kernel,
        "gather",
        (clusters, near, far, *crosses, packed_seed, seed_up, *seed_cross),
        like(labels.shape, F32),
        [stack, total],
    )
    tail_rows = rows // 96 * 16
    head = like((rows - tail_rows, classes), BF16)
    tail = like((tail_rows + 2 * FACTORS, classes), BF16)
    summed, head, squares = call(
        combine_kernel, "combine", (scalars, kept, sent), (packed, head, like((FACTORS, rows), F32))
    )

    head_up = from_up(head)
    head_cross = [from_group(head, step) for step in steps]
    half, half_piece = like((half_rows, classes), BF16), like((half_rows, classes // QUAD), BF16)
    tail, _, current_stack, sums_b, sums_a, *pieces = call(
        mix_kernel,
        "mix",
        (scalars, far, summed, squares, *exchange([squares] * 3), packed_seed),
        (
            tail, packed, like((QUAD * rows, classes // QUAD), BF16),
            half, half, half_piece, half_piece, half_piece,
        ),
    )
    received = exchange(pieces)
    near_total = call(
        near_products,
        "near_products",
        (near, after(current_stack, received[0])),
        like((QUAD * rows, classes // QUAD), F32),
    )
    tail_up = from_up(tail)
    tail_cross = [from_group(after(tail, near_total), step) for step in steps]
    sent_b = from_down(sums_b)
    sums_a = call(pack_kernel, "pack", (scalars, sums_a, *received), half)
    sums_a = after(sums_a, (head_up, head_cross, tail_up, tail_cross))
    sent_a = from_down(sums_a)
    head_up = after(head_up, sums_a)
    triples = [head_up, tail_up, seed_up]
    for top, rest, own in zip(head_cross, tail_cross, seed_cross):
        triples += [top, rest, own]
    _, kept_b, kept_a, *pieces = call(
        gather_mixed_kernel,
        "gather_mixed",
        (clusters, far, *crosses, near_total, *triples),
        (
            like((QUAD * rows, classes // QUAD), F32),
            like(half.shape, F32), half, half_piece, half_piece, half_piece,
        ),
        [pltpu.VMEM(labels.shape, BF16), stack],
        aliases={6: 0},
    )
    received = exchange(pieces)
    sums_b, *pieces = call(add_kernel, "add", (scalars, after(kept_b, received[0]), sent_b), (half, half_piece, half_piece, half_piece))
    kept_a = call(pack_kernel, "pack", (scalars, kept_a, *received), half)
    result = finish(
        finish_b_kernel,
        "finish_b",
        1,
        (scalars, sums_b, *exchange(pieces), seed),
        packed,
        [pltpu.VMEM(half.shape, BF16)],
    )
    return finish(finish_a_kernel, "finish_a", 0, (scalars, result, kept_a, sent_a, seed), packed, aliases={1: 0})


def solution(mesh):
    placed = (P(("grp", "dev"), None), P(("grp", "dev"), None), P(("grp", "dev")))
    return jax.shard_map(
        body, mesh=mesh, in_specs=placed, out_specs=P(("grp", "dev"), None), check_vma=False
    )
```

```python
import functools
import math

import jax
import jax.numpy as jnp
from jax import lax
from jax.experimental import pallas as pl
from jax.experimental.pallas import tpu as pltpu
from jax.sharding import PartitionSpec as P

sharpness = 25.0
keep_share = 0.8
BF16 = jnp.bfloat16
F32 = jnp.float32
QUAD = 4
INVALID = 1e38
FACTORS = 8
MB = 2**20


def along_dev(block, source):
    size = lax.axis_size("dev")
    return lax.ppermute(block, "dev", [(source(i) % size, i) for i in range(size)])


def from_up(block):
    return along_dev(block, lambda i: i + QUAD)


def from_down(block):
    return along_dev(block, lambda i: i - QUAD)


def from_side(block):
    return along_dev(block, lambda i: i ^ 2)


def from_core(block):
    return along_dev(block, lambda i: i ^ 1)


def from_group(block, step):
    size = lax.axis_size("grp")
    return lax.ppermute(block, "grp", [((i + step) % size, i) for i in range(size)])


def after(value, earlier):
    return lax.optimization_barrier((value, earlier))[0]


def exchange(pieces):
    return [along_dev(piece, lambda i, m=m: i ^ m) for m, piece in enumerate(pieces, 1)]


def call(kernel, name, operands, out_shape, scratch=(), limit=12, aliases={}):
    specs = [
        pl.BlockSpec(memory_space=pltpu.SMEM if x.dtype == jnp.int32 else pltpu.VMEM) for x in operands
    ]
    return pl.pallas_call(
        kernel,
        in_specs=specs,
        out_shape=out_shape,
        scratch_shapes=list(scratch),
        input_output_aliases=aliases,
        compiler_params=pltpu.CompilerParams(vmem_limit_bytes=limit * MB),
        name=name,
    )(*operands)


def like(shape, dtype):
    return jax.ShapeDtypeStruct(tuple(shape), dtype)


def dot(left, right):
    return jnp.dot(left, right, preferred_element_type=F32)


def affinity(left, right):
    cosine = lax.dot_general(left, right, (((1,), (1,)), ((), ())), preferred_element_type=F32)
    return jnp.exp2(cosine * (sharpness * math.log2(math.e)))


def cut(block, place, pieces):
    quarter = block.shape[1] // QUAD
    for k in range(QUAD):
        for m, piece in pieces:

            @pl.when(place ^ m == k)
            def _():
                piece[...] = block[:, k * quarter : (k + 1) * quarter]


def join(place, pieces, out):
    quarter = out.shape[1] // QUAD
    for k in range(QUAD):
        for m, piece in pieces:

            @pl.when(place ^ m == k)
            def _():
                out[:, k * quarter : (k + 1) * quarter] = piece[...]


def unit_rows(embeddings):
    values = embeddings.astype(F32)
    scaled = values * lax.rsqrt(jnp.mean(values * values, axis=-1, keepdims=True) + 1e-06)
    return (scaled / math.sqrt(values.shape[-1])).astype(BF16)


def seed_kernel(scalars, labels, seed, *pieces):
    row = lax.broadcasted_iota(jnp.int32, labels.shape, 0)
    seed[...] = jnp.where(row < scalars[1], labels[...].astype(F32), 0.0).astype(BF16)
    cut(seed, scalars[0], list(enumerate(pieces, 1)))


def pack_kernel(scalars, whole, p1, p2, p3, out):
    out[...] = whole[...]
    join(scalars[0], [(1, p1), (2, p2), (3, p3)], out)


def at(cluster, rows):
    return pl.ds(pl.multiple_of(cluster * rows, rows), rows)


def place_units(start, block, stack):
    count = block.shape[0]
    stack[pl.ds(pl.multiple_of(start, count), count), :] = unit_rows(block[...])


def near_kernel(units, near):
    rows = units.shape[0] // QUAD
    for k in range(QUAD):
        for pair in range(2):
            span = slice(2 * pair * rows, 2 * (pair + 1) * rows)
            tile = affinity(units[k * rows : (k + 1) * rows, :], units[span, :])
            if k // 2 == pair:
                row = lax.broadcasted_iota(jnp.int32, tile.shape, 0)
                lane = lax.broadcasted_iota(jnp.int32, tile.shape, 1)
                tile = jnp.where(row + (k % 2) * rows == lane, 0.0, tile)
            near[k * rows : (k + 1) * rows, span] = tile.astype(BF16)


def late_kernel(own, up, p1, p2, p3, late):
    half = late.shape[0] // 2
    late[:half, :] = own[half:, :]
    late[half:, :] = up[half:, :]


def stage_kernel(clusters, own, side_a, core, across_a, units):
    rows = own.shape[0]
    for i, block in enumerate((own, side_a, core, across_a)):
        place_units(clusters[i] * rows, block, units)


def stage_seed_kernel(clusters, own, side_a, core, across_a, seed, units, stack):
    stage_kernel(clusters, own, side_a, core, across_a, units)
    unpack(seed, stack)


def far_kernel(clusters, units_in, up_in, side_b, across_b, stack, units, up_units, far, sums):
    rows = units.shape[0] // QUAD
    half = rows // 2
    for i, block in ((1, side_b), (3, across_b)):
        start = clusters[i] * rows + half
        place_units(start, block.at[:half], units)
        place_units(start, block.at[half:], up_units)
    for k in range(QUAD):
        here = slice(k * rows, (k + 1) * rows)
        for first in range(0, k + 1, 2):
            span = slice(first * rows, min(first + 2, k + 1) * rows)
            far[here, span] = affinity(units[here, :], up_units[span, :]).astype(BF16)
    scatter(far, stack, (sums,))


def unpack(block, stack):
    rows, quarter = stack.shape[0] // QUAD, stack.shape[1]
    for k in range(QUAD):
        stack[k * rows : (k + 1) * rows, :] = block[:, k * quarter : (k + 1) * quarter]


def scatter(far, stack, outs):
    rows, quarter = stack.shape[0] // QUAD, stack.shape[1]
    for k in range(QUAD):
        total = lax.dot_general(
            far[k * rows :, k * rows : (k + 1) * rows],
            stack[k * rows :, :],
            (((0,), (0,)), ((), ())),
            preferred_element_type=F32,
        )
        first = 0
        for out in outs:
            out[:, k * quarter : (k + 1) * quarter] = total[first : first + out.shape[0], :].astype(out.dtype)
            first = first + out.shape[0]


def mix_kernel(scalars, far, summed, s0, s1, s2, s3, seed, tail, mixed, stack, out_b, out_a, p1, p2, p3):
    total = (s0[...] + s1[...]) + (s2[...] + s3[...])
    rows = summed.shape[0]
    kept = tail.shape[0] - 2 * FACTORS
    factor = jnp.where(total > INVALID / 10, 0.0, lax.rsqrt(total / summed.shape[1] + 1e-06))
    high = factor.astype(BF16).astype(F32)
    tail[:kept, :] = summed[rows - kept :, :]
    tail[kept:, :] = jnp.zeros((2 * FACTORS, tail.shape[1]), BF16)
    tail[kept:, :rows] = jnp.concatenate([high, factor - high]).astype(BF16)
    mix(summed.at[: rows - kept], tail, seed, mixed)
    unpack(mixed, stack)
    scatter(far, stack, (out_a, out_b))
    cut(out_a, scalars[0], [(1, p1), (2, p2), (3, p3)])


def cross_kernel(weight, own, *rest):
    others, out = rest[:-1], rest[-1]
    rows = own.shape[0]
    unit = unit_rows(own[...])
    for n, other in enumerate(others):
        out[n * rows : (n + 1) * rows, :] = (affinity(unit, unit_rows(other[...])) * weight).astype(BF16)


def near_products(near, stack, total):
    rows = stack.shape[0] // QUAD
    for k in range(QUAD):
        here = slice(k * rows, (k + 1) * rows)
        total[here, :] = dot(near[here, :], stack[...])


def cross_products(clusters, tiles, n, stack, total):
    rows = stack.shape[0] // QUAD
    for i, tile in enumerate(tiles):
        here = at(clusters[i], rows)
        total[here, :] += dot(tile[n * rows : (n + 1) * rows, :], stack[here, :])


def far_products(far, stack, total, outs):
    rows, quarter = stack.shape[0] // QUAD, stack.shape[1]
    for k in range(QUAD):
        here = slice(k * rows, (k + 1) * rows)
        done = total[here, :] + dot(far[here, : (k + 1) * rows], stack[: (k + 1) * rows, :])
        first = 0
        for out in outs:
            out[:, k * quarter : (k + 1) * quarter] = done[first : first + out.shape[0], :].astype(out.dtype)
            first = first + out.shape[0]


def gather_kernel(clusters, near, far, t0, t1, t2, t3, own, up, *rest):
    cross, (out, stack, total) = rest[:-3], rest[-3:]
    unpack(own, stack)
    near_products(near, stack, total)
    for n, block in enumerate(cross):
        unpack(block, stack)
        cross_products(clusters, (t0, t1, t2, t3), n, stack, total)
    unpack(up, stack)
    far_products(far, stack, total, (out,))


def gather_mixed_kernel(clusters, far, t0, t1, t2, t3, total_in, *rest):
    triples, (total, out_b, out_a, p1, p2, p3, mixed, stack) = rest[:-8], rest[-8:]
    triples = [triples[i : i + 3] for i in range(0, len(triples), 3)]
    for n, triple in enumerate(triples[1:]):
        mix(*triple, mixed)
        unpack(mixed, stack)
        cross_products(clusters, (t0, t1, t2, t3), n, stack, total)
    mix(*triples[0], mixed)
    unpack(mixed, stack)
    far_products(far, stack, total, (out_a, out_b))
    cut(out_a, clusters[0], [(1, p1), (2, p2), (3, p3)])


def lanes_of(count, lanes):
    quarter = lanes // QUAD
    row = lax.broadcasted_iota(jnp.int32, (count, lanes), 0) & (FACTORS - 1)
    lane = lax.broadcasted_iota(jnp.int32, (count, lanes), 1)
    return ((lane >= row * quarter) & (lane < (row + 1) * quarter)).astype(F32).astype(BF16)


def mix(head, tail, seed, out):
    rows, lanes = seed.shape
    first = head.shape[0]
    kept = rows - first
    spread = lax.dot_general(
        tail[kept:, :rows],
        lanes_of(2 * FACTORS, lanes),
        (((0,), (0,)), ((), ())),
        preferred_element_type=F32,
    )
    for block, start, stop in ((head[...], 0, first), (tail[:kept, :], first, rows)):
        share = keep_share * block.astype(F32) * spread[start:stop, :]
        out[start:stop, :] = (share + (1.0 - keep_share) * seed[start:stop, :].astype(F32)).astype(BF16)


def combine_kernel(scalars, kept, sent, summed, head, squares):
    total = kept[...] + sent[...].astype(F32)
    summed[...] = total.astype(BF16)
    head[...] = summed[: head.shape[0], :]
    square = total * total
    high = square.astype(BF16)
    marks = lanes_of(2 * FACTORS, total.shape[1])
    sums = sum(
        lax.dot_general(marks, part, (((1,), (1,)), ((), ())), preferred_element_type=F32)
        for part in (high, (square - high.astype(F32)).astype(BF16))
    )
    row = lax.broadcasted_iota(jnp.int32, sums.shape, 0)
    lane = lax.broadcasted_iota(jnp.int32, sums.shape, 1)
    sums = sums + jnp.where((row == scalars[0]) & (lane >= scalars[1]), INVALID, 0.0)
    squares[...] = sums[:FACTORS, :]


def add_kernel(scalars, kept, sent, out, p1, p2, p3):
    out[...] = (kept[...] + sent[...].astype(F32)).astype(BF16)
    cut(out, scalars[0], [(1, p1), (2, p2), (3, p3)])


def finish_kernel(scalars, kept_a, sent_a, sums_b, p1, p2, p3, seed, out, whole_b):
    whole_b[...] = sums_b[...]
    join(scalars[0], [(1, p1), (2, p2), (3, p3)], whole_b)
    half = kept_a.shape[0]
    for first, summed in (
        (0, kept_a[...].astype(F32) + sent_a[...].astype(F32)),
        (half, whole_b[...].astype(F32)),
    ):
        here = slice(first, first + summed.shape[0])
        factor = lax.rsqrt(jnp.mean(summed * summed, axis=-1, keepdims=True) + 1e-06)
        result = keep_share * summed * factor + (1.0 - keep_share) * seed[here, :].astype(F32)
        row = lax.broadcasted_iota(jnp.int32, summed.shape, 0) + first
        out[here, :] = jnp.where(row < scalars[1], result, 0.0).astype(BF16)


def body(embeddings, labels, cluster_rows):
    rows, classes = labels.shape
    depth = embeddings.shape[1]
    groups = lax.axis_size("grp")
    steps, weight = ([1], 2.0) if groups == 2 else ([1, -1], 1.0)
    place = (lax.axis_index("dev") % QUAD).astype(jnp.int32)
    clusters = jnp.stack([place, place ^ 2, place ^ 1, place ^ 3])
    scalars = jnp.stack([place, cluster_rows[0]])
    stack = pltpu.VMEM((QUAD * rows, classes // QUAD), BF16)
    total = pltpu.VMEM((QUAD * rows, classes // QUAD), F32)
    packed = like(labels.shape, BF16)
    piece = like((rows, classes // QUAD), BF16)
    matrix = like((QUAD * rows, QUAD * rows), BF16)

    half_rows = rows // 2

    own_up = from_up(embeddings)
    side_a = from_side(embeddings[:half_rows])
    seed, *pieces = call(seed_kernel, "seed", (scalars, labels), (packed, piece, piece, piece))
    received = exchange(pieces)
    own_core = from_core(embeddings)
    cross_own = [from_group(after(embeddings, seed), step) for step in steps]
    up_side_a = from_up(side_a)
    late = call(
        late_kernel, "late", (after(embeddings, side_a), own_up, *received), like(embeddings.shape, BF16)
    )
    side_b = from_side(late)
    received[0] = after(received[0], own_up)
    packed_seed = call(pack_kernel, "pack", (scalars, seed, *received), packed)
    seed_up = from_up(packed_seed)
    seed_cross = [from_group(packed_seed, step) for step in steps]
    cross0 = call(
        functools.partial(cross_kernel, weight), "cross", (embeddings, *cross_own), like((len(steps) * rows, rows), BF16)
    )
    across_a = from_core(side_a)
    unit_stack = like((QUAD * rows, depth), BF16)
    units, seed_stack = call(
        stage_seed_kernel,
        "stage_own",
        (clusters, embeddings, side_a, own_core, across_a, packed_seed),
        (unit_stack, like((QUAD * rows, classes // QUAD), BF16)),
    )
    side_b = after(side_b, (cross0, units, up_side_a))
    across_b = from_core(side_b)
    up_core, up_across_a = from_core(own_up), from_core(up_side_a)
    up_units = call(
        stage_kernel, "stage_up", (clusters, after(own_up, side_b), up_side_a, up_core, up_across_a), unit_stack
    )
    cross0 = after(cross0, (side_b, seed_up, seed_cross))
    cross1, cross2 = from_side(cross0), from_core(cross0)
    units, _, far, sums = call(
        far_kernel,
        "far",
        (clusters, units, up_units, side_b, across_b, seed_stack),
        (unit_stack, unit_stack, matrix, packed),
        aliases={1: 0, 2: 1},
    )
    near = call(near_kernel, "near", (units,), matrix)
    cross3 = from_core(after(cross1, near))

    sent = from_down(sums)
    crosses = (cross0, cross1, cross2, cross3)
    kept = call(
        gather_kernel,
        "gather",
        (clusters, near, far, *crosses, packed_seed, seed_up, *seed_cross),
        like(labels.shape, F32),
        [stack, total],
    )
    tail_rows = rows // 96 * 16
    head = like((rows - tail_rows, classes), BF16)
    tail = like((tail_rows + 2 * FACTORS, classes), BF16)
    summed, head, squares = call(
        combine_kernel, "combine", (scalars, kept, sent), (packed, head, like((FACTORS, rows), F32))
    )

    head_up = from_up(head)
    head_cross = [from_group(head, step) for step in steps]
    half, half_piece = like((half_rows, classes), BF16), like((half_rows, classes // QUAD), BF16)
    tail, _, current_stack, sums_b, sums_a, *pieces = call(
        mix_kernel,
        "mix",
        (scalars, far, summed, squares, *exchange([squares] * 3), packed_seed),
        (
            tail, packed, like((QUAD * rows, classes // QUAD), BF16),
            half, half, half_piece, half_piece, half_piece,
        ),
    )
    received = exchange(pieces)
    near_total = call(
        near_products,
        "near_products",
        (near, after(current_stack, received[0])),
        like((QUAD * rows, classes // QUAD), F32),
    )
    tail_up = from_up(tail)
    tail_cross = [from_group(after(tail, near_total), step) for step in steps]
    sent_b = from_down(sums_b)
    sums_a = call(pack_kernel, "pack", (scalars, sums_a, *received), half)
    sums_a = after(sums_a, (head_up, head_cross, tail_up, tail_cross))
    sent_a = from_down(sums_a)
    head_up = after(head_up, sums_a)
    triples = [head_up, tail_up, seed_up]
    for top, rest, own in zip(head_cross, tail_cross, seed_cross):
        triples += [top, rest, own]
    _, kept_b, kept_a, *pieces = call(
        gather_mixed_kernel,
        "gather_mixed",
        (clusters, far, *crosses, near_total, *triples),
        (
            like((QUAD * rows, classes // QUAD), F32),
            like(half.shape, F32), half, half_piece, half_piece, half_piece,
        ),
        [pltpu.VMEM(labels.shape, BF16), stack],
        aliases={6: 0},
    )
    received = exchange(pieces)
    sums_b, *pieces = call(add_kernel, "add", (scalars, after(kept_b, received[0]), sent_b), (half, half_piece, half_piece, half_piece))
    kept_a = call(pack_kernel, "pack", (scalars, kept_a, *received), half)
    return call(
        finish_kernel,
        "finish",
        (scalars, kept_a, sent_a, sums_b, *exchange(pieces), seed),
        packed,
        [pltpu.VMEM(half.shape, BF16)],
    )


def solution(mesh):
    placed = (P(("grp", "dev"), None), P(("grp", "dev"), None), P(("grp", "dev")))
    return jax.shard_map(
        body, mesh=mesh, in_specs=placed, out_specs=P(("grp", "dev"), None), check_vma=False
    )
```

```python
import functools
import math

import jax
import jax.numpy as jnp
from jax import lax
from jax.experimental import pallas as pl
from jax.experimental.pallas import tpu as pltpu
from jax.sharding import PartitionSpec as P

sharpness = 25.0
keep_share = 0.8
BF16 = jnp.bfloat16
F32 = jnp.float32
QUAD = 4
INVALID = 1e38
FACTORS = 8
MB = 2**20


def along_dev(block, source):
    size = lax.axis_size("dev")
    return lax.ppermute(block, "dev", [(source(i) % size, i) for i in range(size)])


def from_up(block):
    return along_dev(block, lambda i: i + QUAD)


def from_down(block):
    return along_dev(block, lambda i: i - QUAD)


def from_side(block):
    return along_dev(block, lambda i: i ^ 2)


def from_core(block):
    return along_dev(block, lambda i: i ^ 1)


def from_group(block, step):
    size = lax.axis_size("grp")
    return lax.ppermute(block, "grp", [((i + step) % size, i) for i in range(size)])


def after(value, earlier):
    return lax.optimization_barrier((value, earlier))[0]


def exchange(pieces):
    return [along_dev(piece, lambda i, m=m: i ^ m) for m, piece in enumerate(pieces, 1)]


def call(kernel, name, operands, out_shape, scratch=(), limit=12, aliases={}):
    specs = [
        pl.BlockSpec(memory_space=pltpu.SMEM if x.dtype == jnp.int32 else pltpu.VMEM) for x in operands
    ]
    return pl.pallas_call(
        kernel,
        in_specs=specs,
        out_shape=out_shape,
        scratch_shapes=list(scratch),
        input_output_aliases=aliases,
        compiler_params=pltpu.CompilerParams(vmem_limit_bytes=limit * MB),
        name=name,
    )(*operands)


def like(shape, dtype):
    return jax.ShapeDtypeStruct(tuple(shape), dtype)


def dot(left, right):
    return jnp.dot(left, right, preferred_element_type=F32)


def affinity(left, right):
    cosine = lax.dot_general(left, right, (((1,), (1,)), ((), ())), preferred_element_type=F32)
    return jnp.exp2(cosine * (sharpness * math.log2(math.e)))


def cut(block, place, pieces):
    quarter = block.shape[1] // QUAD
    for k in range(QUAD):
        for m, piece in pieces:

            @pl.when(place ^ m == k)
            def _():
                piece[...] = block[:, k * quarter : (k + 1) * quarter]


def join(place, pieces, out):
    quarter = out.shape[1] // QUAD
    for k in range(QUAD):
        for m, piece in pieces:

            @pl.when(place ^ m == k)
            def _():
                out[:, k * quarter : (k + 1) * quarter] = piece[...]


def unit_rows(embeddings):
    values = embeddings.astype(F32)
    scaled = values * lax.rsqrt(jnp.mean(values * values, axis=-1, keepdims=True) + 1e-06)
    return (scaled / math.sqrt(values.shape[-1])).astype(BF16)


def seed_kernel(scalars, labels, seed, *pieces):
    row = lax.broadcasted_iota(jnp.int32, labels.shape, 0)
    seed[...] = jnp.where(row < scalars[1], labels[...].astype(F32), 0.0).astype(BF16)
    cut(seed, scalars[0], list(enumerate(pieces, 1)))


def pack_kernel(scalars, whole, p1, p2, p3, out):
    out[...] = whole[...]
    join(scalars[0], [(1, p1), (2, p2), (3, p3)], out)


def at(cluster, rows):
    return pl.ds(pl.multiple_of(cluster * rows, rows), rows)


def place_units(start, block, stack):
    count = block.shape[0]
    stack[pl.ds(pl.multiple_of(start, count), count), :] = unit_rows(block[...])


def near_kernel(units, near):
    rows = units.shape[0] // QUAD
    for k in range(QUAD):
        for pair in range(2):
            span = slice(2 * pair * rows, 2 * (pair + 1) * rows)
            tile = affinity(units[k * rows : (k + 1) * rows, :], units[span, :])
            if k // 2 == pair:
                row = lax.broadcasted_iota(jnp.int32, tile.shape, 0)
                lane = lax.broadcasted_iota(jnp.int32, tile.shape, 1)
                tile = jnp.where(row + (k % 2) * rows == lane, 0.0, tile)
            near[k * rows : (k + 1) * rows, span] = tile.astype(BF16)


def late_kernel(own, up, side, p1, p2, p3, late):
    half = late.shape[0] // 2
    late[:half, :] = own[...]
    late[half:, :] = up[half:, :]


def stage_kernel(clusters, own, side_a, core, across_a, units):
    rows = own.shape[0]
    for i, block in enumerate((own, side_a, core, across_a)):
        place_units(clusters[i] * rows, block, units)


def stage_seed_kernel(clusters, own, side_a, core, across_a, seed, units, stack):
    stage_kernel(clusters, own, side_a, core, across_a, units)
    unpack(seed, stack)


def far_kernel(clusters, units_in, up_in, side_b, across_b, stack, units, up_units, far, sums):
    rows = units.shape[0] // QUAD
    half = rows // 2
    for i, block in ((1, side_b), (3, across_b)):
        start = clusters[i] * rows + half
        place_units(start, block.at[:half], units)
        place_units(start, block.at[half:], up_units)
    for k in range(QUAD):
        here = slice(k * rows, (k + 1) * rows)
        for first in range(0, k + 1, 2):
            span = slice(first * rows, min(first + 2, k + 1) * rows)
            far[here, span] = affinity(units[here, :], up_units[span, :]).astype(BF16)
    scatter(far, stack, (sums,))


def unpack(block, stack):
    rows, quarter = stack.shape[0] // QUAD, stack.shape[1]
    for k in range(QUAD):
        stack[k * rows : (k + 1) * rows, :] = block[:, k * quarter : (k + 1) * quarter]


def scatter(far, stack, outs):
    rows, quarter = stack.shape[0] // QUAD, stack.shape[1]
    for k in range(QUAD):
        total = lax.dot_general(
            far[k * rows :, k * rows : (k + 1) * rows],
            stack[k * rows :, :],
            (((0,), (0,)), ((), ())),
            preferred_element_type=F32,
        )
        first = 0
        for out in outs:
            out[:, k * quarter : (k + 1) * quarter] = total[first : first + out.shape[0], :].astype(out.dtype)
            first = first + out.shape[0]


def mix_kernel(scalars, far, summed, s0, s1, s2, s3, seed, tail, mixed, stack, out_b, out_a, p1, p2, p3):
    total = (s0[...] + s1[...]) + (s2[...] + s3[...])
    rows = summed.shape[0]
    kept = tail.shape[0] - 2 * FACTORS
    factor = jnp.where(total > INVALID / 10, 0.0, lax.rsqrt(total / summed.shape[1] + 1e-06))
    high = factor.astype(BF16).astype(F32)
    tail[:kept, :] = summed[rows - kept :, :]
    tail[kept:, :] = jnp.zeros((2 * FACTORS, tail.shape[1]), BF16)
    tail[kept:, :rows] = jnp.concatenate([high, factor - high]).astype(BF16)
    mix(summed.at[: rows - kept], tail, seed, mixed)
    unpack(mixed, stack)
    scatter(far, stack, (out_a, out_b))
    cut(out_a, scalars[0], [(1, p1), (2, p2), (3, p3)])


def cross_kernel(weight, own, *rest):
    others, out = rest[:-1], rest[-1]
    rows = own.shape[0]
    unit = unit_rows(own[...])
    for n, other in enumerate(others):
        out[n * rows : (n + 1) * rows, :] = (affinity(unit, unit_rows(other[...])) * weight).astype(BF16)


def near_products(near, stack, total):
    rows = stack.shape[0] // QUAD
    for k in range(QUAD):
        here = slice(k * rows, (k + 1) * rows)
        total[here, :] = dot(near[here, :], stack[...])


def cross_products(clusters, tiles, n, stack, total):
    rows = stack.shape[0] // QUAD
    for i, tile in enumerate(tiles):
        here = at(clusters[i], rows)
        total[here, :] += dot(tile[n * rows : (n + 1) * rows, :], stack[here, :])


def far_products(far, stack, total, outs):
    rows, quarter = stack.shape[0] // QUAD, stack.shape[1]
    for k in range(QUAD):
        here = slice(k * rows, (k + 1) * rows)
        done = total[here, :] + dot(far[here, : (k + 1) * rows], stack[: (k + 1) * rows, :])
        first = 0
        for out in outs:
            out[:, k * quarter : (k + 1) * quarter] = done[first : first + out.shape[0], :].astype(out.dtype)
            first = first + out.shape[0]


def gather_kernel(clusters, near, far, t0, t1, t2, t3, own, up, *rest):
    cross, (out, stack, total) = rest[:-3], rest[-3:]
    unpack(own, stack)
    near_products(near, stack, total)
    for n, block in enumerate(cross):
        unpack(block, stack)
        cross_products(clusters, (t0, t1, t2, t3), n, stack, total)
    unpack(up, stack)
    far_products(far, stack, total, (out,))


def gather_mixed_kernel(clusters, far, t0, t1, t2, t3, total_in, *rest):
    triples, (total, out_b, out_a, p1, p2, p3, mixed, stack) = rest[:-8], rest[-8:]
    triples = [triples[i : i + 3] for i in range(0, len(triples), 3)]
    for n, triple in enumerate(triples[1:]):
        mix(*triple, mixed)
        unpack(mixed, stack)
        cross_products(clusters, (t0, t1, t2, t3), n, stack, total)
    mix(*triples[0], mixed)
    unpack(mixed, stack)
    far_products(far, stack, total, (out_a, out_b))
    cut(out_a, clusters[0], [(1, p1), (2, p2), (3, p3)])


def lanes_of(count, lanes):
    quarter = lanes // QUAD
    row = lax.broadcasted_iota(jnp.int32, (count, lanes), 0) & (FACTORS - 1)
    lane = lax.broadcasted_iota(jnp.int32, (count, lanes), 1)
    return ((lane >= row * quarter) & (lane < (row + 1) * quarter)).astype(F32).astype(BF16)


def mix(head, tail, seed, out):
    rows, lanes = seed.shape
    first = head.shape[0]
    kept = rows - first
    spread = lax.dot_general(
        tail[kept:, :rows],
        lanes_of(2 * FACTORS, lanes),
        (((0,), (0,)), ((), ())),
        preferred_element_type=F32,
    )
    for block, start, stop in ((head[...], 0, first), (tail[:kept, :], first, rows)):
        share = keep_share * block.astype(F32) * spread[start:stop, :]
        out[start:stop, :] = (share + (1.0 - keep_share) * seed[start:stop, :].astype(F32)).astype(BF16)


def combine_kernel(scalars, kept, sent, summed, head, squares):
    total = kept[...] + sent[...].astype(F32)
    summed[...] = total.astype(BF16)
    head[...] = summed[: head.shape[0], :]
    square = total * total
    high = square.astype(BF16)
    marks = lanes_of(2 * FACTORS, total.shape[1])
    sums = sum(
        lax.dot_general(marks, part, (((1,), (1,)), ((), ())), preferred_element_type=F32)
        for part in (high, (square - high.astype(F32)).astype(BF16))
    )
    row = lax.broadcasted_iota(jnp.int32, sums.shape, 0)
    lane = lax.broadcasted_iota(jnp.int32, sums.shape, 1)
    sums = sums + jnp.where((row == scalars[0]) & (lane >= scalars[1]), INVALID, 0.0)
    squares[...] = sums[:FACTORS, :]


def add_kernel(scalars, kept, sent, out, p1, p2, p3):
    out[...] = (kept[...] + sent[...].astype(F32)).astype(BF16)
    cut(out, scalars[0], [(1, p1), (2, p2), (3, p3)])


def finish_kernel(scalars, kept_a, sent_a, sums_b, p1, p2, p3, seed, out, whole_b):
    whole_b[...] = sums_b[...]
    join(scalars[0], [(1, p1), (2, p2), (3, p3)], whole_b)
    half = kept_a.shape[0]
    for first, summed in (
        (0, kept_a[...].astype(F32) + sent_a[...].astype(F32)),
        (half, whole_b[...].astype(F32)),
    ):
        here = slice(first, first + summed.shape[0])
        factor = lax.rsqrt(jnp.mean(summed * summed, axis=-1, keepdims=True) + 1e-06)
        result = keep_share * summed * factor + (1.0 - keep_share) * seed[here, :].astype(F32)
        row = lax.broadcasted_iota(jnp.int32, summed.shape, 0) + first
        out[here, :] = jnp.where(row < scalars[1], result, 0.0).astype(BF16)


def body(embeddings, labels, cluster_rows):
    rows, classes = labels.shape
    depth = embeddings.shape[1]
    groups = lax.axis_size("grp")
    steps, weight = ([1], 2.0) if groups == 2 else ([1, -1], 1.0)
    place = (lax.axis_index("dev") % QUAD).astype(jnp.int32)
    clusters = jnp.stack([place, place ^ 2, place ^ 1, place ^ 3])
    scalars = jnp.stack([place, cluster_rows[0]])
    stack = pltpu.VMEM((QUAD * rows, classes // QUAD), BF16)
    total = pltpu.VMEM((QUAD * rows, classes // QUAD), F32)
    packed = like(labels.shape, BF16)
    piece = like((rows, classes // QUAD), BF16)
    matrix = like((QUAD * rows, QUAD * rows), BF16)

    half_rows = rows // 2

    own_up = from_up(embeddings)
    side_a = from_side(embeddings[:half_rows])
    seed, *pieces = call(seed_kernel, "seed", (scalars, labels), (packed, piece, piece, piece))
    received = exchange(pieces)
    own_core = from_core(embeddings)
    cross_own = [from_group(after(embeddings, seed), step) for step in steps]
    up_side_a = from_up(side_a)
    late = call(
        late_kernel, "late", (after(embeddings, side_a)[half_rows:], own_up, side_a, *received), like(embeddings.shape, BF16)
    )
    side_b = from_side(late)
    received[0] = after(received[0], own_up)
    packed_seed = call(pack_kernel, "pack", (scalars, seed, *received), packed)
    seed_up = from_up(packed_seed)
    seed_cross = [from_group(packed_seed, step) for step in steps]
    cross0 = call(
        functools.partial(cross_kernel, weight), "cross", (embeddings, *cross_own), like((len(steps) * rows, rows), BF16)
    )
    across_a = from_core(side_a)
    unit_stack = like((QUAD * rows, depth), BF16)
    units, seed_stack = call(
        stage_seed_kernel,
        "stage_own",
        (clusters, embeddings, side_a, own_core, across_a, packed_seed),
        (unit_stack, like((QUAD * rows, classes // QUAD), BF16)),
    )
    up_core, up_across_a = from_core(own_up), from_core(up_side_a)
    side_b = after(side_b, (cross0, units, up_across_a))
    across_b = from_core(side_b)
    up_units = call(
        stage_kernel, "stage_up", (clusters, after(own_up, side_b), up_side_a, up_core, up_across_a), unit_stack
    )
    cross0 = after(cross0, (side_b, seed_up, seed_cross))
    cross1, cross2 = from_side(cross0), from_core(cross0)
    units, _, far, sums = call(
        far_kernel,
        "far",
        (clusters, units, up_units, side_b, across_b, seed_stack),
        (unit_stack, unit_stack, matrix, packed),
        aliases={1: 0, 2: 1},
    )
    near = call(near_kernel, "near", (units,), matrix)
    cross3 = from_core(after(cross1, near))

    sent = from_down(sums)
    crosses = (cross0, cross1, cross2, cross3)
    kept = call(
        gather_kernel,
        "gather",
        (clusters, near, far, *crosses, packed_seed, seed_up, *seed_cross),
        like(labels.shape, F32),
        [stack, total],
    )
    tail_rows = rows // 96 * 16
    head = like((rows - tail_rows, classes), BF16)
    tail = like((tail_rows + 2 * FACTORS, classes), BF16)
    summed, head, squares = call(
        combine_kernel, "combine", (scalars, kept, sent), (packed, head, like((FACTORS, rows), F32))
    )

    head_up = from_up(head)
    head_cross = [from_group(head, step) for step in steps]
    half, half_piece = like((half_rows, classes), BF16), like((half_rows, classes // QUAD), BF16)
    tail, _, current_stack, sums_b, sums_a, *pieces = call(
        mix_kernel,
        "mix",
        (scalars, far, summed, squares, *exchange([squares] * 3), packed_seed),
        (
            tail, packed, like((QUAD * rows, classes // QUAD), BF16),
            half, half, half_piece, half_piece, half_piece,
        ),
    )
    received = exchange(pieces)
    near_total = call(
        near_products,
        "near_products",
        (near, after(current_stack, received[0])),
        like((QUAD * rows, classes // QUAD), F32),
    )
    tail_up = from_up(tail)
    tail_cross = [from_group(after(tail, near_total), step) for step in steps]
    sent_b = from_down(sums_b)
    sums_a = call(pack_kernel, "pack", (scalars, sums_a, *received), half)
    sums_a = after(sums_a, (head_up, head_cross, tail_up, tail_cross))
    sent_a = from_down(sums_a)
    head_up = after(head_up, sums_a)
    triples = [head_up, tail_up, seed_up]
    for top, rest, own in zip(head_cross, tail_cross, seed_cross):
        triples += [top, rest, own]
    _, kept_b, kept_a, *pieces = call(
        gather_mixed_kernel,
        "gather_mixed",
        (clusters, far, *crosses, near_total, *triples),
        (
            like((QUAD * rows, classes // QUAD), F32),
            like(half.shape, F32), half, half_piece, half_piece, half_piece,
        ),
        [pltpu.VMEM(labels.shape, BF16), stack],
        aliases={6: 0},
    )
    received = exchange(pieces)
    sums_b, *pieces = call(add_kernel, "add", (scalars, after(kept_b, received[0]), sent_b), (half, half_piece, half_piece, half_piece))
    kept_a = call(pack_kernel, "pack", (scalars, kept_a, *received), half)
    return call(
        finish_kernel,
        "finish",
        (scalars, kept_a, sent_a, sums_b, *exchange(pieces), seed),
        packed,
        [pltpu.VMEM(half.shape, BF16)],
    )


def solution(mesh):
    placed = (P(("grp", "dev"), None), P(("grp", "dev"), None), P(("grp", "dev")))
    return jax.shard_map(
        body, mesh=mesh, in_specs=placed, out_specs=P(("grp", "dev"), None), check_vma=False
    )
```

```python
import functools
import math

import jax
import jax.numpy as jnp
from jax import lax
from jax.experimental import pallas as pl
from jax.experimental.pallas import tpu as pltpu
from jax.sharding import PartitionSpec as P

sharpness = 25.0
keep_share = 0.8
BF16 = jnp.bfloat16
F32 = jnp.float32
QUAD = 4
INVALID = 1e38
FACTORS = 8
MB = 2**20


def along_dev(block, source):
    size = lax.axis_size("dev")
    return lax.ppermute(block, "dev", [(source(i) % size, i) for i in range(size)])


def from_up(block):
    return along_dev(block, lambda i: i + QUAD)


def from_down(block):
    return along_dev(block, lambda i: i - QUAD)


def from_side(block):
    return along_dev(block, lambda i: i ^ 2)


def from_core(block):
    return along_dev(block, lambda i: i ^ 1)


def from_group(block, step):
    size = lax.axis_size("grp")
    return lax.ppermute(block, "grp", [((i + step) % size, i) for i in range(size)])


def after(value, earlier):
    return lax.optimization_barrier((value, earlier))[0]


def exchange(pieces):
    return [along_dev(piece, lambda i, m=m: i ^ m) for m, piece in enumerate(pieces, 1)]


def call(kernel, name, operands, out_shape, scratch=(), limit=12, aliases={}):
    specs = [
        pl.BlockSpec(memory_space=pltpu.SMEM if x.dtype == jnp.int32 else pltpu.VMEM) for x in operands
    ]
    return pl.pallas_call(
        kernel,
        in_specs=specs,
        out_shape=out_shape,
        scratch_shapes=list(scratch),
        input_output_aliases=aliases,
        compiler_params=pltpu.CompilerParams(vmem_limit_bytes=limit * MB),
        name=name,
    )(*operands)


def like(shape, dtype):
    return jax.ShapeDtypeStruct(tuple(shape), dtype)


def dot(left, right):
    return jnp.dot(left, right, preferred_element_type=F32)


def affinity(left, right):
    cosine = lax.dot_general(left, right, (((1,), (1,)), ((), ())), preferred_element_type=F32)
    return jnp.exp2(cosine * (sharpness * math.log2(math.e)))


def cut(block, place, pieces):
    quarter = block.shape[1] // QUAD
    for k in range(QUAD):
        for m, piece in pieces:

            @pl.when(place ^ m == k)
            def _():
                piece[...] = block[:, k * quarter : (k + 1) * quarter]


def join(place, pieces, out):
    quarter = out.shape[1] // QUAD
    for k in range(QUAD):
        for m, piece in pieces:

            @pl.when(place ^ m == k)
            def _():
                out[:, k * quarter : (k + 1) * quarter] = piece[...]


def unit_rows(embeddings):
    values = embeddings.astype(F32)
    scaled = values * lax.rsqrt(jnp.mean(values * values, axis=-1, keepdims=True) + 1e-06)
    return (scaled / math.sqrt(values.shape[-1])).astype(BF16)


def seed_kernel(scalars, labels, seed, *pieces):
    row = lax.broadcasted_iota(jnp.int32, labels.shape, 0)
    seed[...] = jnp.where(row < scalars[1], labels[...].astype(F32), 0.0).astype(BF16)
    cut(seed, scalars[0], list(enumerate(pieces, 1)))


def pack_kernel(scalars, whole, p1, p2, p3, out):
    out[...] = whole[...]
    join(scalars[0], [(1, p1), (2, p2), (3, p3)], out)


def at(cluster, rows):
    return pl.ds(pl.multiple_of(cluster * rows, rows), rows)


def place_units(start, block, stack):
    count = block.shape[0]
    stack[pl.ds(pl.multiple_of(start, count), count), :] = unit_rows(block[...])


def near_kernel(units, near):
    rows = units.shape[0] // QUAD
    for k in range(QUAD):
        for pair in range(2):
            span = slice(2 * pair * rows, 2 * (pair + 1) * rows)
            tile = affinity(units[k * rows : (k + 1) * rows, :], units[span, :])
            if k // 2 == pair:
                row = lax.broadcasted_iota(jnp.int32, tile.shape, 0)
                lane = lax.broadcasted_iota(jnp.int32, tile.shape, 1)
                tile = jnp.where(row + (k % 2) * rows == lane, 0.0, tile)
            near[k * rows : (k + 1) * rows, span] = tile.astype(BF16)


def late_kernel(own, up, side, p1, p2, p3, late):
    half = late.shape[0] // 2
    late[:half, :] = own[...]
    late[half:, :] = up[half:, :]


def stage_kernel(clusters, own, side_a, core, across_a, units):
    rows = own.shape[0]
    for i, block in enumerate((own, side_a, core, across_a)):
        place_units(clusters[i] * rows, block, units)


def stage_seed_kernel(clusters, own, side_a, core, across_a, seed, units, stack):
    stage_kernel(clusters, own, side_a, core, across_a, units)
    unpack(seed, stack)


def far_kernel(clusters, units_in, up_in, side_b, across_b, stack, units, up_units, far, sums):
    rows = units.shape[0] // QUAD
    half = rows // 2
    for i, block in ((1, side_b), (3, across_b)):
        start = clusters[i] * rows + half
        place_units(start, block.at[:half], units)
        place_units(start, block.at[half:], up_units)
    for k in range(QUAD):
        here = slice(k * rows, (k + 1) * rows)
        for first in range(0, k + 1, 2):
            span = slice(first * rows, min(first + 2, k + 1) * rows)
            far[here, span] = affinity(units[here, :], up_units[span, :]).astype(BF16)
    scatter(far, stack, (sums,))


def unpack(block, stack):
    rows, quarter = stack.shape[0] // QUAD, stack.shape[1]
    for k in range(QUAD):
        stack[k * rows : (k + 1) * rows, :] = block[:, k * quarter : (k + 1) * quarter]


def scatter(far, stack, outs):
    rows, quarter = stack.shape[0] // QUAD, stack.shape[1]
    for k in range(QUAD):
        total = lax.dot_general(
            far[k * rows :, k * rows : (k + 1) * rows],
            stack[k * rows :, :],
            (((0,), (0,)), ((), ())),
            preferred_element_type=F32,
        )
        first = 0
        for out in outs:
            out[:, k * quarter : (k + 1) * quarter] = total[first : first + out.shape[0], :].astype(out.dtype)
            first = first + out.shape[0]


def mix_kernel(scalars, far, summed, s0, s1, s2, s3, seed, tail, mixed, stack, out_b, out_a, p1, p2, p3):
    total = (s0[...] + s1[...]) + (s2[...] + s3[...])
    rows = summed.shape[0]
    kept = tail.shape[0] - 2 * FACTORS
    factor = jnp.where(total > INVALID / 10, 0.0, lax.rsqrt(total / summed.shape[1] + 1e-06))
    high = factor.astype(BF16).astype(F32)
    tail[:kept, :] = summed[rows - kept :, :]
    tail[kept:, :] = jnp.zeros((2 * FACTORS, tail.shape[1]), BF16)
    tail[kept:, :rows] = jnp.concatenate([high, factor - high]).astype(BF16)
    mix(summed.at[: rows - kept], tail, seed, mixed)
    unpack(mixed, stack)
    scatter(far, stack, (out_a, out_b))
    cut(out_a, scalars[0], [(1, p1), (2, p2), (3, p3)])


def cross_kernel(weight, own, *rest):
    others, out = rest[:-1], rest[-1]
    rows = own.shape[0]
    unit = unit_rows(own[...])
    for n, other in enumerate(others):
        out[n * rows : (n + 1) * rows, :] = (affinity(unit, unit_rows(other[...])) * weight).astype(BF16)


def near_products(near, stack, total):
    rows = stack.shape[0] // QUAD
    for k in range(QUAD):
        here = slice(k * rows, (k + 1) * rows)
        total[here, :] = dot(near[here, :], stack[...])


def cross_products(clusters, tiles, n, stack, total):
    rows = stack.shape[0] // QUAD
    for i, tile in enumerate(tiles):
        here = at(clusters[i], rows)
        total[here, :] += dot(tile[n * rows : (n + 1) * rows, :], stack[here, :])


def far_products(far, stack, total, outs):
    rows, quarter = stack.shape[0] // QUAD, stack.shape[1]
    for k in range(QUAD):
        here = slice(k * rows, (k + 1) * rows)
        done = total[here, :] + dot(far[here, : (k + 1) * rows], stack[: (k + 1) * rows, :])
        first = 0
        for out in outs:
            out[:, k * quarter : (k + 1) * quarter] = done[first : first + out.shape[0], :].astype(out.dtype)
            first = first + out.shape[0]


def gather_kernel(clusters, near, far, t0, t1, t2, t3, own, up, *rest):
    cross, (out, stack, total) = rest[:-3], rest[-3:]
    unpack(own, stack)
    near_products(near, stack, total)
    for n, block in enumerate(cross):
        unpack(block, stack)
        cross_products(clusters, (t0, t1, t2, t3), n, stack, total)
    unpack(up, stack)
    far_products(far, stack, total, (out,))


def gather_mixed_kernel(clusters, far, t0, t1, t2, t3, total_in, *rest):
    triples, (total, out_b, out_a, p1, p2, p3, mixed, stack) = rest[:-8], rest[-8:]
    triples = [triples[i : i + 3] for i in range(0, len(triples), 3)]
    for n, triple in enumerate(triples[1:]):
        mix(*triple, mixed)
        unpack(mixed, stack)
        cross_products(clusters, (t0, t1, t2, t3), n, stack, total)
    mix(*triples[0], mixed)
    unpack(mixed, stack)
    far_products(far, stack, total, (out_a, out_b))
    cut(out_a, clusters[0], [(1, p1), (2, p2), (3, p3)])


def lanes_of(count, lanes):
    quarter = lanes // QUAD
    row = lax.broadcasted_iota(jnp.int32, (count, lanes), 0) & (FACTORS - 1)
    lane = lax.broadcasted_iota(jnp.int32, (count, lanes), 1)
    return ((lane >= row * quarter) & (lane < (row + 1) * quarter)).astype(F32).astype(BF16)


def mix(head, tail, seed, out):
    rows, lanes = seed.shape
    first = head.shape[0]
    kept = rows - first
    spread = lax.dot_general(
        tail[kept:, :rows],
        lanes_of(2 * FACTORS, lanes),
        (((0,), (0,)), ((), ())),
        preferred_element_type=F32,
    )
    for block, start, stop in ((head[...], 0, first), (tail[:kept, :], first, rows)):
        share = keep_share * block.astype(F32) * spread[start:stop, :]
        out[start:stop, :] = (share + (1.0 - keep_share) * seed[start:stop, :].astype(F32)).astype(BF16)


def combine_kernel(scalars, kept, sent, summed, head, squares):
    total = kept[...] + sent[...].astype(F32)
    summed[...] = total.astype(BF16)
    head[...] = summed[: head.shape[0], :]
    square = total * total
    high = square.astype(BF16)
    marks = lanes_of(2 * FACTORS, total.shape[1])
    sums = sum(
        lax.dot_general(marks, part, (((1,), (1,)), ((), ())), preferred_element_type=F32)
        for part in (high, (square - high.astype(F32)).astype(BF16))
    )
    row = lax.broadcasted_iota(jnp.int32, sums.shape, 0)
    lane = lax.broadcasted_iota(jnp.int32, sums.shape, 1)
    sums = sums + jnp.where((row == scalars[0]) & (lane >= scalars[1]), INVALID, 0.0)
    squares[...] = sums[:FACTORS, :]


def add_kernel(scalars, kept, sent, out, p1, p2, p3):
    out[...] = (kept[...] + sent[...].astype(F32)).astype(BF16)
    cut(out, scalars[0], [(1, p1), (2, p2), (3, p3)])


def finish_kernel(scalars, kept_a, sent_a, sums_b, p1, p2, p3, seed, out, whole_b):
    whole_b[...] = sums_b[...]
    join(scalars[0], [(1, p1), (2, p2), (3, p3)], whole_b)
    half = kept_a.shape[0]
    for first, summed in (
        (0, kept_a[...].astype(F32) + sent_a[...].astype(F32)),
        (half, whole_b[...].astype(F32)),
    ):
        here = slice(first, first + summed.shape[0])
        factor = lax.rsqrt(jnp.mean(summed * summed, axis=-1, keepdims=True) + 1e-06)
        result = keep_share * summed * factor + (1.0 - keep_share) * seed[here, :].astype(F32)
        row = lax.broadcasted_iota(jnp.int32, summed.shape, 0) + first
        out[here, :] = jnp.where(row < scalars[1], result, 0.0).astype(BF16)


def body(embeddings, labels, cluster_rows):
    rows, classes = labels.shape
    depth = embeddings.shape[1]
    groups = lax.axis_size("grp")
    steps, weight = ([1], 2.0) if groups == 2 else ([1, -1], 1.0)
    place = (lax.axis_index("dev") % QUAD).astype(jnp.int32)
    clusters = jnp.stack([place, place ^ 2, place ^ 1, place ^ 3])
    scalars = jnp.stack([place, cluster_rows[0]])
    stack = pltpu.VMEM((QUAD * rows, classes // QUAD), BF16)
    total = pltpu.VMEM((QUAD * rows, classes // QUAD), F32)
    packed = like(labels.shape, BF16)
    piece = like((rows, classes // QUAD), BF16)
    matrix = like((QUAD * rows, QUAD * rows), BF16)

    half_rows = rows // 2

    own_up = from_up(embeddings)
    side_a = from_side(embeddings[:half_rows])
    seed, *pieces = call(seed_kernel, "seed", (scalars, labels), (packed, piece, piece, piece))
    received = exchange(pieces)
    own_core = from_core(embeddings)
    cross_own = [from_group(after(embeddings, seed), step) for step in steps]
    up_side_a = from_up(side_a)
    late = call(
        late_kernel, "late", (after(embeddings, side_a)[half_rows:], own_up, side_a, *received), like(embeddings.shape, BF16)
    )
    side_b = from_side(late)
    received[0] = after(received[0], own_up)
    packed_seed = call(pack_kernel, "pack", (scalars, seed, *received), packed)
    seed_up = from_up(packed_seed)
    seed_cross = [from_group(packed_seed, step) for step in steps]
    across_a = from_core(side_a)
    unit_stack = like((QUAD * rows, depth), BF16)
    units, seed_stack = call(
        stage_seed_kernel,
        "stage_own",
        (clusters, embeddings, side_a, own_core, across_a, packed_seed),
        (unit_stack, like((QUAD * rows, classes // QUAD), BF16)),
    )
    cross0 = call(
        functools.partial(cross_kernel, weight), "cross", (after(embeddings, units), *cross_own), like((len(steps) * rows, rows), BF16)
    )
    up_core, up_across_a = from_core(own_up), from_core(up_side_a)
    side_b = after(side_b, (cross0, units, up_across_a))
    across_b = from_core(side_b)
    up_units = call(
        stage_kernel, "stage_up", (clusters, after(own_up, side_b), up_side_a, up_core, up_across_a), unit_stack
    )
    cross0 = after(cross0, (side_b, seed_up, seed_cross))
    cross1, cross2 = from_side(cross0), from_core(cross0)
    units, _, far, sums = call(
        far_kernel,
        "far",
        (clusters, units, up_units, side_b, across_b, seed_stack),
        (unit_stack, unit_stack, matrix, packed),
        aliases={1: 0, 2: 1},
    )
    near = call(near_kernel, "near", (units,), matrix)
    cross3 = from_core(after(cross1, near))

    sent = from_down(sums)
    crosses = (cross0, cross1, cross2, cross3)
    kept = call(
        gather_kernel,
        "gather",
        (clusters, near, far, *crosses, packed_seed, seed_up, *seed_cross),
        like(labels.shape, F32),
        [stack, total],
    )
    tail_rows = rows // 96 * 16
    head = like((rows - tail_rows, classes), BF16)
    tail = like((tail_rows + 2 * FACTORS, classes), BF16)
    summed, head, squares = call(
        combine_kernel, "combine", (scalars, kept, sent), (packed, head, like((FACTORS, rows), F32))
    )

    head_up = from_up(head)
    head_cross = [from_group(head, step) for step in steps]
    half, half_piece = like((half_rows, classes), BF16), like((half_rows, classes // QUAD), BF16)
    tail, _, current_stack, sums_b, sums_a, *pieces = call(
        mix_kernel,
        "mix",
        (scalars, far, summed, squares, *exchange([squares] * 3), packed_seed),
        (
            tail, packed, like((QUAD * rows, classes // QUAD), BF16),
            half, half, half_piece, half_piece, half_piece,
        ),
    )
    received = exchange(pieces)
    near_total = call(
        near_products,
        "near_products",
        (near, after(current_stack, received[0])),
        like((QUAD * rows, classes // QUAD), F32),
    )
    tail_up = from_up(tail)
    tail_cross = [from_group(after(tail, near_total), step) for step in steps]
    sent_b = from_down(sums_b)
    sums_a = call(pack_kernel, "pack", (scalars, sums_a, *received), half)
    sums_a = after(sums_a, (head_up, head_cross, tail_up, tail_cross))
    sent_a = from_down(sums_a)
    head_up = after(head_up, sums_a)
    triples = [head_up, tail_up, seed_up]
    for top, rest, own in zip(head_cross, tail_cross, seed_cross):
        triples += [top, rest, own]
    _, kept_b, kept_a, *pieces = call(
        gather_mixed_kernel,
        "gather_mixed",
        (clusters, far, *crosses, near_total, *triples),
        (
            like((QUAD * rows, classes // QUAD), F32),
            like(half.shape, F32), half, half_piece, half_piece, half_piece,
        ),
        [pltpu.VMEM(labels.shape, BF16), stack],
        aliases={6: 0},
    )
    received = exchange(pieces)
    sums_b, *pieces = call(add_kernel, "add", (scalars, after(kept_b, received[0]), sent_b), (half, half_piece, half_piece, half_piece))
    kept_a = call(pack_kernel, "pack", (scalars, kept_a, *received), half)
    return call(
        finish_kernel,
        "finish",
        (scalars, kept_a, sent_a, sums_b, *exchange(pieces), seed),
        packed,
        [pltpu.VMEM(half.shape, BF16)],
    )


def solution(mesh):
    placed = (P(("grp", "dev"), None), P(("grp", "dev"), None), P(("grp", "dev")))
    return jax.shard_map(
        body, mesh=mesh, in_specs=placed, out_specs=P(("grp", "dev"), None), check_vma=False
    )
```

```python
import functools
import math

import jax
import jax.numpy as jnp
from jax import lax
from jax.experimental import pallas as pl
from jax.experimental.pallas import tpu as pltpu
from jax.sharding import PartitionSpec as P

sharpness = 25.0
keep_share = 0.8
BF16 = jnp.bfloat16
F32 = jnp.float32
QUAD = 4
INVALID = 1e38
FACTORS = 8
MB = 2**20


def along_dev(block, source):
    size = lax.axis_size("dev")
    return lax.ppermute(block, "dev", [(source(i) % size, i) for i in range(size)])


def from_up(block):
    return along_dev(block, lambda i: i + QUAD)


def from_down(block):
    return along_dev(block, lambda i: i - QUAD)


def from_side(block):
    return along_dev(block, lambda i: i ^ 2)


def from_core(block):
    return along_dev(block, lambda i: i ^ 1)


def from_group(block, step):
    size = lax.axis_size("grp")
    return lax.ppermute(block, "grp", [((i + step) % size, i) for i in range(size)])


def after(value, earlier):
    return lax.optimization_barrier((value, earlier))[0]


def exchange(pieces):
    return [along_dev(piece, lambda i, m=m: i ^ m) for m, piece in enumerate(pieces, 1)]


def call(kernel, name, operands, out_shape, scratch=(), limit=12, aliases={}):
    specs = [
        pl.BlockSpec(memory_space=pltpu.SMEM if x.dtype == jnp.int32 else pltpu.VMEM) for x in operands
    ]
    return pl.pallas_call(
        kernel,
        in_specs=specs,
        out_shape=out_shape,
        scratch_shapes=list(scratch),
        input_output_aliases=aliases,
        compiler_params=pltpu.CompilerParams(vmem_limit_bytes=limit * MB),
        name=name,
    )(*operands)


def like(shape, dtype):
    return jax.ShapeDtypeStruct(tuple(shape), dtype)


def dot(left, right):
    return jnp.dot(left, right, preferred_element_type=F32)


def affinity(left, right):
    cosine = lax.dot_general(left, right, (((1,), (1,)), ((), ())), preferred_element_type=F32)
    return jnp.exp2(cosine * (sharpness * math.log2(math.e)))


def cut(block, place, pieces):
    quarter = block.shape[1] // QUAD
    for k in range(QUAD):
        for m, piece in pieces:

            @pl.when(place ^ m == k)
            def _():
                piece[...] = block[:, k * quarter : (k + 1) * quarter]


def join(place, pieces, out):
    quarter = out.shape[1] // QUAD
    for k in range(QUAD):
        for m, piece in pieces:

            @pl.when(place ^ m == k)
            def _():
                out[:, k * quarter : (k + 1) * quarter] = piece[...]


def unit_rows(embeddings):
    values = embeddings.astype(F32)
    scaled = values * lax.rsqrt(jnp.mean(values * values, axis=-1, keepdims=True) + 1e-06)
    return (scaled / math.sqrt(values.shape[-1])).astype(BF16)


def seed_kernel(scalars, labels, seed, *pieces):
    row = lax.broadcasted_iota(jnp.int32, labels.shape, 0)
    seed[...] = jnp.where(row < scalars[1], labels[...].astype(F32), 0.0).astype(BF16)
    cut(seed, scalars[0], list(enumerate(pieces, 1)))


def pack_kernel(scalars, whole, p1, p2, p3, out):
    out[...] = whole[...]
    join(scalars[0], [(1, p1), (2, p2), (3, p3)], out)


def at(cluster, rows):
    return pl.ds(pl.multiple_of(cluster * rows, rows), rows)


def place_units(start, block, stack):
    count = block.shape[0]
    stack[pl.ds(pl.multiple_of(start, count), count), :] = unit_rows(block[...])


def near_kernel(units, near):
    rows = units.shape[0] // QUAD
    for k in range(QUAD):
        for pair in range(2):
            span = slice(2 * pair * rows, 2 * (pair + 1) * rows)
            tile = affinity(units[k * rows : (k + 1) * rows, :], units[span, :])
            if k // 2 == pair:
                row = lax.broadcasted_iota(jnp.int32, tile.shape, 0)
                lane = lax.broadcasted_iota(jnp.int32, tile.shape, 1)
                tile = jnp.where(row + (k % 2) * rows == lane, 0.0, tile)
            near[k * rows : (k + 1) * rows, span] = tile.astype(BF16)


def late_kernel(own, up, side, p1, p2, p3, late):
    half = late.shape[0] // 2
    late[:half, :] = own[...]
    late[half:, :] = up[half:, :]


def stage_kernel(clusters, own, side_a, core, across_a, units):
    rows = own.shape[0]
    for i, block in enumerate((own, side_a, core, across_a)):
        place_units(clusters[i] * rows, block, units)


def stage_seed_kernel(clusters, own, side_a, core, across_a, seed, units, stack):
    stage_kernel(clusters, own, side_a, core, across_a, units)
    unpack(seed, stack)


def far_kernel(clusters, units_in, up_in, side_b, across_b, stack, units, up_units, far, sums):
    rows = units.shape[0] // QUAD
    half = rows // 2
    for i, block in ((1, side_b), (3, across_b)):
        start = clusters[i] * rows + half
        place_units(start, block.at[:half], units)
        place_units(start, block.at[half:], up_units)
    for k in range(QUAD):
        here = slice(k * rows, (k + 1) * rows)
        for first in range(0, k + 1, 2):
            span = slice(first * rows, min(first + 2, k + 1) * rows)
            far[here, span] = affinity(units[here, :], up_units[span, :]).astype(BF16)
    scatter(far, stack, (sums,))


def unpack(block, stack):
    rows, quarter = stack.shape[0] // QUAD, stack.shape[1]
    for k in range(QUAD):
        stack[k * rows : (k + 1) * rows, :] = block[:, k * quarter : (k + 1) * quarter]


def scatter(far, stack, outs):
    rows, quarter = stack.shape[0] // QUAD, stack.shape[1]
    for k in range(QUAD):
        total = lax.dot_general(
            far[k * rows :, k * rows : (k + 1) * rows],
            stack[k * rows :, :],
            (((0,), (0,)), ((), ())),
            preferred_element_type=F32,
        )
        first = 0
        for out in outs:
            out[:, k * quarter : (k + 1) * quarter] = total[first : first + out.shape[0], :].astype(out.dtype)
            first = first + out.shape[0]


def mix_kernel(scalars, far, summed, s0, s1, s2, s3, seed, tail, mixed, stack, out_b, out_a, p1, p2, p3):
    total = (s0[...] + s1[...]) + (s2[...] + s3[...])
    rows = summed.shape[0]
    kept = tail.shape[0] - 2 * FACTORS
    factor = jnp.where(total > INVALID / 10, 0.0, lax.rsqrt(total / summed.shape[1] + 1e-06))
    high = factor.astype(BF16).astype(F32)
    tail[:kept, :] = summed[rows - kept :, :]
    tail[kept:, :] = jnp.zeros((2 * FACTORS, tail.shape[1]), BF16)
    tail[kept:, :rows] = jnp.concatenate([high, factor - high]).astype(BF16)
    mix(summed.at[: rows - kept], tail, seed, mixed)
    unpack(mixed, stack)
    scatter(far, stack, (out_a, out_b))
    cut(out_a, scalars[0], [(1, p1), (2, p2), (3, p3)])


def cross_kernel(weight, own, *rest):
    others, out = rest[:-1], rest[-1]
    rows = own.shape[0]
    unit = unit_rows(own[...])
    for n, other in enumerate(others):
        out[n * rows : (n + 1) * rows, :] = (affinity(unit, unit_rows(other[...])) * weight).astype(BF16)


def near_products(near, stack, total):
    rows = stack.shape[0] // QUAD
    for k in range(QUAD):
        here = slice(k * rows, (k + 1) * rows)
        total[here, :] = dot(near[here, :], stack[...])


def cross_products(clusters, tiles, n, stack, total):
    rows = stack.shape[0] // QUAD
    for i, tile in enumerate(tiles):
        here = at(clusters[i], rows)
        total[here, :] += dot(tile[n * rows : (n + 1) * rows, :], stack[here, :])


def far_products(far, stack, total, outs):
    rows, quarter = stack.shape[0] // QUAD, stack.shape[1]
    for k in range(QUAD):
        here = slice(k * rows, (k + 1) * rows)
        done = total[here, :] + dot(far[here, : (k + 1) * rows], stack[: (k + 1) * rows, :])
        first = 0
        for out in outs:
            out[:, k * quarter : (k + 1) * quarter] = done[first : first + out.shape[0], :].astype(out.dtype)
            first = first + out.shape[0]


def gather_kernel(clusters, near, far, t0, t1, t2, t3, own, up, *rest):
    cross, (out, stack, total) = rest[:-3], rest[-3:]
    unpack(own, stack)
    near_products(near, stack, total)
    for n, block in enumerate(cross):
        unpack(block, stack)
        cross_products(clusters, (t0, t1, t2, t3), n, stack, total)
    unpack(up, stack)
    far_products(far, stack, total, (out,))


def gather_mixed_kernel(clusters, far, t0, t1, t2, t3, total_in, *rest):
    triples, (total, out_b, out_a, p1, p2, p3, mixed, stack) = rest[:-8], rest[-8:]
    triples = [triples[i : i + 3] for i in range(0, len(triples), 3)]
    for n, triple in enumerate(triples[1:]):
        mix(*triple, mixed)
        unpack(mixed, stack)
        cross_products(clusters, (t0, t1, t2, t3), n, stack, total)
    mix(*triples[0], mixed)
    unpack(mixed, stack)
    far_products(far, stack, total, (out_a, out_b))
    cut(out_a, clusters[0], [(1, p1), (2, p2), (3, p3)])


def lanes_of(count, lanes):
    quarter = lanes // QUAD
    row = lax.broadcasted_iota(jnp.int32, (count, lanes), 0) & (FACTORS - 1)
    lane = lax.broadcasted_iota(jnp.int32, (count, lanes), 1)
    return ((lane >= row * quarter) & (lane < (row + 1) * quarter)).astype(F32).astype(BF16)


def mix(head, tail, seed, out):
    rows, lanes = seed.shape
    first = head.shape[0]
    kept = rows - first
    spread = lax.dot_general(
        tail[kept:, :rows],
        lanes_of(2 * FACTORS, lanes),
        (((0,), (0,)), ((), ())),
        preferred_element_type=F32,
    )
    for block, start, stop in ((head[...], 0, first), (tail[:kept, :], first, rows)):
        share = keep_share * block.astype(F32) * spread[start:stop, :]
        out[start:stop, :] = (share + (1.0 - keep_share) * seed[start:stop, :].astype(F32)).astype(BF16)


def combine_kernel(scalars, kept, sent, summed, head, squares):
    total = kept[...] + sent[...].astype(F32)
    summed[...] = total.astype(BF16)
    head[...] = summed[: head.shape[0], :]
    square = total * total
    high = square.astype(BF16)
    marks = lanes_of(2 * FACTORS, total.shape[1])
    sums = sum(
        lax.dot_general(marks, part, (((1,), (1,)), ((), ())), preferred_element_type=F32)
        for part in (high, (square - high.astype(F32)).astype(BF16))
    )
    row = lax.broadcasted_iota(jnp.int32, sums.shape, 0)
    lane = lax.broadcasted_iota(jnp.int32, sums.shape, 1)
    sums = sums + jnp.where((row == scalars[0]) & (lane >= scalars[1]), INVALID, 0.0)
    squares[...] = sums[:FACTORS, :]


def add_kernel(scalars, kept, sent, out, p1, p2, p3):
    out[...] = (kept[...] + sent[...].astype(F32)).astype(BF16)
    cut(out, scalars[0], [(1, p1), (2, p2), (3, p3)])


def finish_kernel(scalars, kept_a, sent_a, sums_b, p1, p2, p3, seed, out, whole_b):
    whole_b[...] = sums_b[...]
    join(scalars[0], [(1, p1), (2, p2), (3, p3)], whole_b)
    half = kept_a.shape[0]
    for first, summed in (
        (0, kept_a[...].astype(F32) + sent_a[...].astype(F32)),
        (half, whole_b[...].astype(F32)),
    ):
        here = slice(first, first + summed.shape[0])
        factor = lax.rsqrt(jnp.mean(summed * summed, axis=-1, keepdims=True) + 1e-06)
        result = keep_share * summed * factor + (1.0 - keep_share) * seed[here, :].astype(F32)
        row = lax.broadcasted_iota(jnp.int32, summed.shape, 0) + first
        out[here, :] = jnp.where(row < scalars[1], result, 0.0).astype(BF16)


def body(embeddings, labels, cluster_rows):
    rows, classes = labels.shape
    depth = embeddings.shape[1]
    groups = lax.axis_size("grp")
    steps, weight = ([1], 2.0) if groups == 2 else ([1, -1], 1.0)
    place = (lax.axis_index("dev") % QUAD).astype(jnp.int32)
    clusters = jnp.stack([place, place ^ 2, place ^ 1, place ^ 3])
    scalars = jnp.stack([place, cluster_rows[0]])
    stack = pltpu.VMEM((QUAD * rows, classes // QUAD), BF16)
    total = pltpu.VMEM((QUAD * rows, classes // QUAD), F32)
    packed = like(labels.shape, BF16)
    piece = like((rows, classes // QUAD), BF16)
    matrix = like((QUAD * rows, QUAD * rows), BF16)

    half_rows = rows // 2

    own_up = from_up(embeddings)
    side_a = from_side(embeddings[:half_rows])
    seed, *pieces = call(seed_kernel, "seed", (scalars, labels), (packed, piece, piece, piece))
    received = exchange(pieces)
    own_core = from_core(embeddings)
    cross_own = [from_group(after(embeddings, seed), step) for step in steps]
    up_side_a = from_up(side_a)
    late = call(
        late_kernel, "late", (after(embeddings, side_a)[half_rows:], own_up, side_a, *received), like(embeddings.shape, BF16)
    )
    side_b = from_side(late)
    received[0] = after(received[0], own_up)
    packed_seed = call(pack_kernel, "pack", (scalars, seed, *received), packed)
    seed_up = from_up(packed_seed)
    seed_cross = [from_group(packed_seed, step) for step in steps]
    cross0 = call(
        functools.partial(cross_kernel, weight), "cross", (embeddings, *cross_own), like((len(steps) * rows, rows), BF16)
    )
    across_a = from_core(side_a)
    unit_stack = like((QUAD * rows, depth), BF16)
    units, seed_stack = call(
        stage_seed_kernel,
        "stage_own",
        (clusters, embeddings, side_a, own_core, across_a, packed_seed),
        (unit_stack, like((QUAD * rows, classes // QUAD), BF16)),
    )
    up_core, up_across_a = from_core(own_up), from_core(up_side_a)
    side_b = after(side_b, (cross0, units, up_across_a))
    across_b = from_core(side_b)
    up_units = call(
        stage_kernel, "stage_up", (clusters, after(own_up, side_b), up_side_a, up_core, up_across_a), unit_stack
    )
    cross0 = after(cross0, (side_b, seed_up, seed_cross))
    cross1, cross2 = from_side(cross0), from_core(cross0)
    units, _, far, sums = call(
        far_kernel,
        "far",
        (clusters, units, up_units, side_b, across_b, seed_stack),
        (unit_stack, unit_stack, matrix, packed),
        aliases={1: 0, 2: 1},
    )
    near = call(near_kernel, "near", (units,), matrix)
    cross3 = from_core(after(cross1, near))

    sent = from_down(sums)
    crosses = (cross0, cross1, cross2, cross3)
    kept = call(
        gather_kernel,
        "gather",
        (clusters, near, far, *crosses, packed_seed, seed_up, *seed_cross),
        like(labels.shape, F32),
        [stack, total],
    )
    tail_rows = rows // 96 * 16
    head = like((rows - tail_rows, classes), BF16)
    tail = like((tail_rows + 2 * FACTORS, classes), BF16)
    summed, head, squares = call(
        combine_kernel, "combine", (scalars, kept, sent), (packed, head, like((FACTORS, rows), F32))
    )

    head_up = from_up(head)
    head_cross = [from_group(head, step) for step in steps]
    last_rows = rows * 11 // 24 // 16 * 16
    part_a, part_b = like((rows - last_rows, classes), BF16), like((last_rows, classes), BF16)
    piece_a, piece_b = (like((p.shape[0], classes // QUAD), BF16) for p in (part_a, part_b))
    tail, _, current_stack, sums_b, sums_a, *pieces = call(
        mix_kernel,
        "mix",
        (scalars, far, summed, squares, *exchange([squares] * 3), packed_seed),
        (
            tail, packed, like((QUAD * rows, classes // QUAD), BF16),
            part_b, part_a, piece_a, piece_a, piece_a,
        ),
    )
    received = exchange(pieces)
    near_total = call(
        near_products,
        "near_products",
        (near, after(current_stack, received[0])),
        like((QUAD * rows, classes // QUAD), F32),
    )
    tail_up = from_up(tail)
    tail_cross = [from_group(after(tail, near_total), step) for step in steps]
    sent_b = from_down(sums_b)
    sums_a = call(pack_kernel, "pack", (scalars, sums_a, *received), part_a)
    sums_a = after(sums_a, (head_up, head_cross, tail_up, tail_cross))
    sent_a = from_down(sums_a)
    head_up = after(head_up, sums_a)
    triples = [head_up, tail_up, seed_up]
    for top, rest, own in zip(head_cross, tail_cross, seed_cross):
        triples += [top, rest, own]
    _, kept_b, kept_a, *pieces = call(
        gather_mixed_kernel,
        "gather_mixed",
        (clusters, far, *crosses, near_total, *triples),
        (
            like((QUAD * rows, classes // QUAD), F32),
            like(part_b.shape, F32), part_a, piece_a, piece_a, piece_a,
        ),
        [pltpu.VMEM(labels.shape, BF16), stack],
        aliases={6: 0},
    )
    received = exchange(pieces)
    sums_b, *pieces = call(add_kernel, "add", (scalars, after(kept_b, received[0]), sent_b), (part_b, piece_b, piece_b, piece_b))
    kept_a = call(pack_kernel, "pack", (scalars, kept_a, *received), part_a)
    return call(
        finish_kernel,
        "finish",
        (scalars, kept_a, sent_a, sums_b, *exchange(pieces), seed),
        packed,
        [pltpu.VMEM(part_b.shape, BF16)],
    )


def solution(mesh):
    placed = (P(("grp", "dev"), None), P(("grp", "dev"), None), P(("grp", "dev")))
    return jax.shard_map(
        body, mesh=mesh, in_specs=placed, out_specs=P(("grp", "dev"), None), check_vma=False
    )
```
